512 devices in a mesh: coef: 32 (over z, x_lo), band: 16 (over x_hi, y, core).
Axes of the slice: x: 4 (x_hi: 2, x_lo: 2; x = x_hi * 2 + x_lo), y: 4, z: 16, core: 2. Of those that a mesh axis runs over, the one named last changes fastest.
Arguments:
- wave: bfloat16 [4096, 131072], P('band', 'coef')
- projector: bfloat16 [512, 131072], P('band', 'coef'), may hold values from -0.015625 to 0.015625
- gvec: int32 [3, 131072], P(None, 'coef'), may hold values from -13 to 13, as said below
- atom_of: int32 [512], replicated, may hold values from 0 to 63, never falling along the last dimension, each value on 1 to 16 neighbouring positions
- dion: bfloat16 [512, 512], replicated
- qaug: bfloat16 [512, 512], replicated, as said below
Outputs:
- precond_resid: bfloat16 [4096, 131072], P('band', 'coef')
The draws below stay inside these ranges and needn't reach their ends.
Inputs may be any that keep to these rules, and one draw needn't show every extreme that they name: `gvec`: no component is zero. `qaug`: within any set of at most 16 projectors, each diagonal entry exceeds both the sum of magnitudes of the other entries of its row and that of its column in that set.
All inputs are finite; a program needn't handle non-finite values.
Results may differ from the reference program's by a relative error of at most 0.0047.
Values may be sent and summed in bfloat16 or wider, within the bound.
No kernel may reach another device: no remote copies, remote signals or barrier semaphores. Data moves between devices by JAX's collectives and lax.ppermute only.
A program may use at most 64 MiB of HBM per device.

```python
import math
import jax
import jax.numpy as jnp
import numpy as np
from jax import lax

NG = 131072
NP = 512
NATOM = 64
BLOCK_MOST = 16
BAND_DEV = 256
NB = 4096
N_BAND = 16


def draw_wave(key, part):
    key = jax.random.fold_in(key, 1)
    key_rows, key_base = jax.random.split(key, 2)
    rows = 0.1 * jnp.exp(jax.random.uniform(key_rows, (NB, 1), jnp.float32) * jnp.log(10.0))
    place = jnp.arange(NG, dtype=jnp.float32) / NG
    amp = jnp.power(10.0, -place)[None, :]
    base = jax.random.truncated_normal(key_base, -4.0, 4.0, (NB, NG), jnp.float32)
    return (rows * amp * base).astype(jnp.bfloat16)


def draw_gvec(key, part):
    key = jax.random.fold_in(key, 2)
    key_mag, key_sign = jax.random.split(key)
    index = jnp.arange(NG, dtype=jnp.int32)
    reach = 2 + 12 * index // NG
    mags = jax.random.randint(key_mag, (3, NG), 1, reach[None, :] + 1)
    signs = 2 * jax.random.randint(key_sign, (3, NG), 0, 2) - 1
    return (mags * signs).astype(jnp.int32)


def draw_dion(key, part):
    key = jax.random.fold_in(key, 3)
    key_off, key_diag = jax.random.split(key)
    off = jax.random.uniform(key_off, (NP, NP), jnp.float32, -2.0, 2.0)
    diag = jax.random.uniform(key_diag, (NP,), jnp.float32, 4.0, 8.0)
    eye = jnp.arange(NP)[:, None] == jnp.arange(NP)[None, :]
    return jnp.where(eye, diag[None, :], off).astype(jnp.bfloat16)


def draw_qaug(key, part):
    key = jax.random.fold_in(key, 4)
    key_off, key_diag = jax.random.split(key)
    off = jax.random.uniform(key_off, (NP, NP), jnp.float32, -0.5, 0.5)
    diag = jax.random.uniform(key_diag, (NP,), jnp.float32, 9.0, 12.0)
    eye = jnp.arange(NP)[:, None] == jnp.arange(NP)[None, :]
    return jnp.where(eye, diag[None, :], off).astype(jnp.bfloat16)


def block_levels(rng, extent, pieces, smallest, high):
    level, own = 1.0, jax.random.fold_in(rng, 6)
    for axis_at, shards_of in pieces:
        heights = jnp.exp(jax.random.uniform(jax.random.fold_in(own, axis_at), (shards_of,), jnp.float32, smallest / len(pieces), high / len(pieces)))
        level = level * jnp.repeat(heights, extent[axis_at] // shards_of).reshape([-1 if axis == axis_at else 1 for axis in range(len(extent))])
    return level


def profile(amount, total, most, skew):
    portions = [(1 << 20) // math.isqrt(standing ** skew) + 1 for standing in range(2, amount + 1)]
    rest, holding = total - most - (amount - 1), [1] * (amount - 1)
    while rest > 0:
        movable = [i for i in range(amount - 1) if holding[i] < most]
        pool, budget = sum([portions[i] for i in movable]), rest
        for i in movable:
            addition = min(most - holding[i], max(1, budget * portions[i] // pool), rest)
            holding[i] = holding[i] + addition
            rest = rest - addition
    return np.array([most] + holding)


def uneven_parts(stream_key, amount, total, bound, slope):
    if amount == 2:
        one = jax.random.randint(stream_key, (), max(1, total - bound), min(bound, total - 1) + 1)
        return jnp.stack([one, total - one])
    lengths = jnp.asarray(profile(amount, total, bound, slope), jnp.int32)
    couples = (amount - 1) // 2
    source_of, taker = lengths[1:1 + 2 * couples:2], lengths[2:2 + 2 * couples:2]
    room = jnp.minimum(source_of - 1, bound - taker)
    shifted = jax.random.randint(jax.random.fold_in(stream_key, 1), (couples,), 0, 1 << 20) % (room + 1)
    lengths = lengths.at[1:1 + 2 * couples:2].set(source_of - shifted).at[2:2 + 2 * couples:2].set(taker + shifted)
    return lengths[jax.random.permutation(jax.random.fold_in(stream_key, 2), amount)]


def bell_draw(rng, dims, deviation, limit, cuts=(), kind=jnp.bfloat16):
    array = jax.random.normal(rng, dims, jnp.float32) * deviation
    if len(cuts) > 0:
        array = block_levels(rng, dims, cuts, -0.22, 0.18) * array
    return jnp.clip(array, min=-limit, max=limit).astype(kind)


def setup_inputs(seed: int = 0) -> dict:
    key_of = jax.random.split(jax.random.key(seed), 7)
    wave = draw_wave(jax.random.fold_in(key_of[6], 71), 0)
    projector = bell_draw(key_of[1], (NP, NG), NG ** -0.5, 0.015625, ((0, 16), (1, 32)))
    gvec = draw_gvec(jax.random.fold_in(key_of[6], 71), 0)
    atom_of = jnp.searchsorted(jnp.cumsum(uneven_parts(key_of[3], NATOM, NP, BLOCK_MOST, 0)), jnp.arange(NP), side="right").astype(jnp.int32)
    dion = draw_dion(jax.random.fold_in(key_of[6], 71), 0)
    qaug = draw_qaug(jax.random.fold_in(key_of[6], 71), 0)
    return {"wave": wave, "projector": projector, "gvec": gvec, "atom_of": atom_of, "dion": dion, "qaug": qaug}


kinetic_unit = 0.005


def kinetic(gvec):
    comps = gvec.astype(jnp.float32)
    return kinetic_unit * jnp.sum(comps * comps, axis=0)


def masked(atom_of, dion, qaug):
    same = atom_of[:, None] == atom_of[None, :]
    dmask = jnp.where(same, dion.astype(jnp.float32), jnp.float32(0.0))
    qmask = jnp.where(same, qaug.astype(jnp.float32), jnp.float32(0.0))
    return dmask, qmask


def couple(intersection, sq, ksq, dmask, qmask):
    pd = jnp.dot(intersection, dmask, precision=lax.Precision.HIGHEST)
    pq = jnp.dot(intersection, qmask, precision=lax.Precision.HIGHEST)
    energy = (ksq + jnp.sum(intersection * pd, axis=1)) / (sq + jnp.sum(intersection * pq, axis=1))
    ekin = ksq / (sq + 1e-6)
    coupled = (pd - energy[:, None] * pq).astype(jnp.bfloat16)
    return coupled, energy, ekin


def finish(wave, kin, expanded, energy, ekin):
    wavef = wave.astype(jnp.float32)
    resid = (kin[None, :] - energy[:, None]) * wavef + expanded
    ratio = kin[None, :] / ekin[:, None]
    num = 27.0 + ratio * (18.0 + ratio * (12.0 + 8.0 * ratio))
    return (num / (num + 16.0 * ratio ** 4) * resid).astype(jnp.bfloat16)


def reference(wave, projector, gvec, atom_of, dion, qaug):
    kin = kinetic(gvec)
    dmask, qmask = masked(atom_of, dion, qaug)

    def one_block(block):
        wavef = block.astype(jnp.float32)
        sq = jnp.sum(wavef * wavef, axis=1)
        ksq = jnp.sum(kin[None, :] * wavef * wavef, axis=1)
        intersection = jnp.dot(block, projector.T, preferred_element_type=jnp.float32)
        coupled, energy, ekin = couple(intersection, sq, ksq, dmask, qmask)
        expanded = jnp.dot(coupled, projector, preferred_element_type=jnp.float32)
        return finish(block, kin, expanded, energy, ekin)

    blocks = wave.reshape(N_BAND, BAND_DEV, NG)
    return lax.map(one_block, blocks).reshape(NB, NG)
```

```python
import functools
import jax
import jax.numpy as jnp
from jax import lax
from jax.experimental import pallas as pl
from jax.experimental.pallas import tpu as pltpu
from jax.sharding import PartitionSpec as P

kinetic_unit = 0.005
f32 = jnp.float32
bf16 = jnp.bfloat16

N_COEF = 32
N_BAND = 16
ROWS = 256
COLS = 4096
NPROJ = 512
SHARD = NPROJ // N_BAND
HALF_PROJ = NPROJ // 2
QUARTER_PROJ = NPROJ // 4
NEAR = 8
BANDS = ROWS // NEAR
STAT_ROWS = BANDS // 4
NEAR_ROWS = 2 * BANDS + STAT_ROWS
FAR_ROWS = BANDS + STAT_ROWS
N_Z_HI = N_COEF // NEAR
FAR = 2 * N_Z_HI

anywhere = pl.BlockSpec(memory_space=pl.ANY)
vmem = pl.BlockSpec(memory_space=pltpu.VMEM)
smem = pl.BlockSpec(memory_space=pltpu.SMEM)

CORE, Z_HI, ORDER = 0, 1, 2


def in_vmem(value):
    return pltpu.with_memory_space_constraint(value, pltpu.VMEM)


def in_hbm(value):
    return pltpu.with_memory_space_constraint(value, pltpu.HBM)


def params(mib):
    return pltpu.CompilerParams(vmem_limit_bytes=mib * 1024 * 1024)


def cost(flops, bytes_accessed):
    return pl.CostEstimate(flops=flops, bytes_accessed=bytes_accessed, transcendentals=0)


def pieces(value):
    hi = value.astype(bf16).astype(f32)
    rest = value - hi
    mid = rest.astype(bf16).astype(f32)
    lo = (rest - mid).astype(bf16).astype(f32)
    return hi, mid, lo


def stat_lanes():
    return lax.broadcasted_iota(jnp.int32, (STAT_ROWS, HALF_PROJ), 1)


def split_rows(value):
    lane = stat_lanes() & 63
    hi, mid, lo = [jnp.where((lane == 0) | (lane == 3), piece, 0.0) for piece in pieces(value)]
    return hi + pltpu.roll(mid, 1, 1) + pltpu.roll(lo, 2, 1)


def join_rows(packed):
    return packed + pltpu.roll(packed, HALF_PROJ - 1, 1) + pltpu.roll(packed, HALF_PROJ - 2, 1)


def to_rows(first, second):
    lane = stat_lanes()
    out = jnp.zeros((STAT_ROWS, HALF_PROJ), f32)
    for k in range(4):
        rows = slice(k * STAT_ROWS, (k + 1) * STAT_ROWS)
        out = jnp.where(lane == 64 * k, first[rows], jnp.where(lane == 64 * k + 3, second[rows], out))
    return split_rows(out)


def from_rows(packed):
    lane = stat_lanes()
    columns = []
    for begin in (0, 3):
        columns.append(jnp.concatenate([
            jnp.sum(jnp.where((lane >= 64 * k + begin) & (lane < 64 * k + begin + 3), packed, 0.0), axis=1, keepdims=True)
            for k in range(4)
        ], axis=0))
    return columns


def kinetic(gvec):
    comps = gvec.astype(f32)
    return kinetic_unit * (comps[0:1] * comps[0:1] + comps[1:2] * comps[1:2] + comps[2:3] * comps[2:3])


def stats_kernel(wave, gvec, stat, wave_v, sems):
    copies = [
        pltpu.make_async_copy(
            wave.at[pl.ds(n * BANDS, BANDS), :], wave_v.at[pl.ds(n * BANDS, BANDS), :], sems.at[n])
        for n in range(NEAR)
    ]
    for copy in copies:
        copy.start()
    kin = kinetic(gvec[...])
    for n, copy in enumerate(copies):
        copy.wait()
        value = wave_v[n * BANDS:(n + 1) * BANDS, :].astype(f32)
        square = value * value
        sq = jnp.sum(square, axis=1, keepdims=True)
        ksq = jnp.sum(square * kin, axis=1, keepdims=True)
        stat[n * STAT_ROWS:(n + 1) * STAT_ROWS, :] = to_rows(sq, ksq)


def stats(wave, gvec):
    return pl.pallas_call(
        stats_kernel,
        in_specs=[anywhere, vmem],
        out_specs=[vmem, vmem],
        out_shape=[
            jax.ShapeDtypeStruct((NEAR * STAT_ROWS, HALF_PROJ), f32),
            pltpu.VMEM((ROWS, COLS), bf16),
        ],
        scratch_shapes=[pltpu.SemaphoreType.DMA((NEAR,))],
        compiler_params=params(16),
        cost_estimate=cost(5 * ROWS * COLS, 2 * ROWS * COLS),
        name="stats",
    )(in_hbm(wave), gvec)


def weights_kernel(atom_of, dion, qaug, out):
    number = lax.broadcasted_iota(jnp.int32, (64, NPROJ), 0)
    member = jnp.where(atom_of[...] == number, 1.0, 0.0).astype(bf16)
    same = lax.dot_general(member, member, (((0,), (0,)), ((), ())), preferred_element_type=f32) > 0.5
    to = lax.broadcasted_iota(jnp.int32, (NPROJ, NPROJ), 0)
    source = ((to & 0xE0) << 1) | ((to >> 8) << 5) | (to & 31)
    order = jnp.where(source == lax.broadcasted_iota(jnp.int32, (NPROJ, NPROJ), 1), 1.0, 0.0).astype(bf16)
    for at, matrix in enumerate((dion, qaug)):
        value = jnp.where(same, matrix[...].astype(f32), 0.0).astype(bf16)
        rows = jnp.dot(order, value, preferred_element_type=f32).astype(bf16)
        out[:, at * NPROJ:(at + 1) * NPROJ] = lax.dot_general(
            rows, order, (((1,), (1,)), ((), ())), preferred_element_type=f32).astype(bf16)


def masked_weights(atom_of, dion, qaug):
    return pl.pallas_call(
        weights_kernel,
        in_specs=[vmem] * 3,
        out_specs=vmem,
        out_shape=jax.ShapeDtypeStruct((NPROJ, 2 * NPROJ), bf16),
        compiler_params=params(24),
        cost_estimate=cost(9 * NPROJ ** 3, 8 * NPROJ * NPROJ),
        name="masked_weights",
    )(atom_of.reshape(1, NPROJ), dion, qaug)


def against(left, right):
    return lax.dot_general(left, right, (((1,), (1,)), ((), ())), preferred_element_type=f32)


N_SHARDS = HALF_PROJ // SHARD


def intersect_kernel(place, stat, wave_own, wave_other, *refs):
    shards = refs[:N_SHARDS]
    message, whole, whole_v, message_v, out_sem = refs[N_SHARDS:]
    for i, shard in enumerate(shards):
        at = pl.multiple_of(place[ORDER + i] * SHARD, SHARD)
        whole_v[pl.ds(at, SHARD), :] = shard[...]
    back = pltpu.make_async_copy(whole_v, whole, out_sem)
    back.start()
    for core, wave in enumerate((wave_own, wave_other)):
        total = against(wave[...], whole_v[...])
        for n in range(NEAR):
            at = n * NEAR_ROWS + core * BANDS
            message_v[at:at + BANDS, :] = total[n * BANDS:(n + 1) * BANDS]
    for n in range(NEAR):
        at = n * NEAR_ROWS + 2 * BANDS
        message_v[at:at + STAT_ROWS, :] = stat[n * STAT_ROWS:(n + 1) * STAT_ROWS, :]
    message[...] = message_v[...].astype(bf16)
    back.wait()


def intersect(place, stat, wave_own, wave_other, shards):
    return pl.pallas_call(
        intersect_kernel,
        in_specs=[smem] + [vmem] * (3 + N_SHARDS),
        out_specs=[vmem, anywhere],
        out_shape=[
            jax.ShapeDtypeStruct((NEAR * NEAR_ROWS, HALF_PROJ), bf16),
            pltpu.HBM((HALF_PROJ, COLS), bf16),
        ],
        scratch_shapes=[
            pltpu.VMEM((HALF_PROJ, COLS), bf16),
            pltpu.VMEM((NEAR * NEAR_ROWS, HALF_PROJ), f32),
            pltpu.SemaphoreType.DMA,
        ],
        compiler_params=params(24),
        cost_estimate=cost(4 * ROWS * COLS * HALF_PROJ, 2 * (2 * ROWS + 2 * HALF_PROJ) * COLS),
        name="intersect",
    )(place, stat, in_vmem(wave_own), in_vmem(wave_other), *[in_vmem(shard) for shard in shards])


def near_sum_kernel(place, received, keep, message, message_v):
    total = jnp.sum(received[...].astype(f32).reshape(NEAR, NEAR_ROWS, HALF_PROJ), axis=0)
    keep[...] = total[:BANDS]
    rows = split_rows(join_rows(total[2 * BANDS:]))
    core = place[CORE]
    for zh in range(N_Z_HI):
        for c, value in ((core, total[:BANDS]), (1 - core, total[BANDS:2 * BANDS])):
            at = pl.multiple_of((zh * 2 + c) * FAR_ROWS, STAT_ROWS)
            message_v[pl.ds(at, BANDS), :] = value
            message_v[pl.ds(at + BANDS, STAT_ROWS), :] = rows
    message[...] = message_v[...].astype(bf16)


def near_sum(place, received):
    return pl.pallas_call(
        near_sum_kernel,
        in_specs=[smem, vmem],
        out_specs=[vmem, vmem],
        out_shape=[
            jax.ShapeDtypeStruct((BANDS, HALF_PROJ), f32),
            jax.ShapeDtypeStruct((FAR * FAR_ROWS, HALF_PROJ), bf16),
        ],
        scratch_shapes=[pltpu.VMEM((FAR * FAR_ROWS, HALF_PROJ), f32)],
        compiler_params=params(16),
        cost_estimate=cost(NEAR * NEAR_ROWS * HALF_PROJ, 3 * NEAR * NEAR_ROWS * HALF_PROJ),
        name="near_sum",
    )(place, received)


def couple_kernel(place, keep, received, weights, out):
    blocks = received[...].astype(f32).reshape(FAR, FAR_ROWS, HALF_PROJ)
    core = place[CORE]
    own_at = place[Z_HI] * 2 + core
    halves, packed = [], []
    for c in range(2):
        total = jnp.zeros((BANDS, HALF_PROJ), f32)
        rows = jnp.zeros((STAT_ROWS, HALF_PROJ), f32)
        for zh in range(N_Z_HI):
            block = blocks[zh * 2 + c]
            total += jnp.where(own_at == zh * 2 + c, keep[...], block[:BANDS])
            rows += block[BANDS:]
        halves.append(total)
        packed.append(rows)
    inter = jnp.concatenate(halves, axis=1)
    sq, ksq = from_rows(jnp.where(core == 0, packed[0], packed[1]))
    stacked = jnp.concatenate(pieces(inter), axis=0).astype(bf16)
    both = jnp.dot(stacked, weights[...], preferred_element_type=f32)
    both = both[:BANDS] + (both[BANDS:2 * BANDS] + both[2 * BANDS:])
    pd, pq = both[:, :NPROJ], both[:, NPROJ:]
    energy = (ksq + jnp.sum(inter * pd, axis=1, keepdims=True)) / (
        sq + jnp.sum(inter * pq, axis=1, keepdims=True))
    ekin = ksq / (sq + 1e-6)
    coupled = pd - energy * pq
    block = jnp.concatenate([coupled[:, :HALF_PROJ], coupled[:, HALF_PROJ:], to_rows(energy, ekin)], axis=0)
    out[...] = jnp.concatenate([block] * NEAR, axis=0).astype(bf16)


def couple(place, keep, received, weights):
    return pl.pallas_call(
        couple_kernel,
        in_specs=[smem] + [vmem] * 3,
        out_specs=vmem,
        out_shape=jax.ShapeDtypeStruct((NEAR * NEAR_ROWS, HALF_PROJ), bf16),
        compiler_params=params(16),
        cost_estimate=cost(12 * BANDS * NPROJ * NPROJ, 4 * NPROJ * NPROJ + 4 * ROWS * NPROJ),
        name="couple",
    )(place, keep, received, weights)


TILE = 256
N_TILES = COLS // TILE
CHUNK = 16


def finish_kernel(place, coupled, gvec, wave, whole_own, whole_other, out,
                  own_v, other_v, out_v, halves_v, energy_v, scale_v, even_v, odd_v, sems, out_sems):
    def columns(tile):
        return pl.ds(pl.multiple_of(tile * TILE, TILE), TILE)

    def copies(tile):
        cols = columns(tile)
        return [
            pltpu.make_async_copy(whole_own.at[:, cols], own_v.at[:, cols], sems.at[tile, 0]),
            pltpu.make_async_copy(whole_other.at[:, cols], other_v.at[:, cols], sems.at[tile, 1]),
        ]

    def out_copy(tile):
        cols = columns(tile)
        return pltpu.make_async_copy(out_v.at[:, cols], out.at[:, cols], out_sems.at[tile])

    def arrive(tile):
        for copy in copies(tile):
            copy.wait()

    def expand(tile, expanded_v):
        cols = columns(tile)
        expanded_v[...] = jnp.dot(halves_v[:ROWS, :], own_v[:, cols], preferred_element_type=f32) + jnp.dot(
            halves_v[ROWS:, :], other_v[:, cols], preferred_element_type=f32)

    def conclude(tile, expanded_v):
        cols = columns(tile)
        kin = jnp.broadcast_to(kinetic(gvec[:, cols]), (CHUNK, TILE))
        for i in range(ROWS // CHUNK):
            rows = slice(i * CHUNK, (i + 1) * CHUNK)
            energy = jnp.concatenate([energy_v[rows, :]] * (TILE // 128), axis=1)
            scale = jnp.concatenate([scale_v[rows, :]] * (TILE // 128), axis=1)
            resid = (kin - energy) * wave[rows, cols].astype(f32) + expanded_v[rows, :]
            u = kin * scale
            v = u * u
            num = (1.0 + u) * (1.0 + v)
            inverse = pl.reciprocal(num + 3.0 * (v * v), approx=True)
            out_v[rows, cols] = ((num * inverse) * resid).astype(bf16)

    for tile in range(N_TILES):
        for copy in copies(tile):
            copy.start()
    core = place[CORE]
    blocks = coupled[...].astype(f32).reshape(NEAR, NEAR_ROWS, HALF_PROJ)
    for n in range(NEAR):
        rows = slice(n * BANDS, (n + 1) * BANDS)
        first, second = blocks[n, :BANDS].astype(bf16), blocks[n, BANDS:2 * BANDS].astype(bf16)
        halves_v[rows, :] = jnp.where(core == 0, first, second)
        halves_v[ROWS + n * BANDS:ROWS + (n + 1) * BANDS, :] = jnp.where(core == 0, second, first)
        energy, ekin = from_rows(blocks[n, 2 * BANDS:])
        energy_v[rows, :] = jnp.broadcast_to(energy, (BANDS, 128))
        scale_v[rows, :] = jnp.broadcast_to((2.0 / 3.0) / ekin, (BANDS, 128))
    arrive(0)
    expand(0, even_v)

    @pl.loop(0, N_TILES // 2)
    def _(i):
        arrive(2 * i + 1)

        @pl.when(i + 1 < N_TILES // 2)
        def _():
            arrive(2 * i + 2)

        expand(2 * i + 1, odd_v)
        conclude(2 * i, even_v)
        out_copy(2 * i).start()
        expand(jnp.minimum(2 * i + 2, N_TILES - 1), even_v)
        conclude(2 * i + 1, odd_v)
        out_copy(2 * i + 1).start()

    for tile in range(N_TILES):
        out_copy(tile).wait()


def finish(place, coupled, wave, gvec, whole_own, whole_other):
    return pl.pallas_call(
        finish_kernel,
        in_specs=[smem] + [vmem] * 3 + [anywhere] * 2,
        out_specs=anywhere,
        out_shape=jax.ShapeDtypeStruct((ROWS, COLS), bf16),
        scratch_shapes=[pltpu.VMEM((HALF_PROJ, COLS), bf16)] * 2
        + [pltpu.VMEM((ROWS, COLS), bf16), pltpu.VMEM((2 * ROWS, HALF_PROJ), bf16)]
        + [pltpu.VMEM((ROWS, 128), f32)] * 2 + [pltpu.VMEM((ROWS, TILE), f32)] * 2
        + [pltpu.SemaphoreType.DMA((N_TILES, 2)), pltpu.SemaphoreType.DMA((N_TILES,))],
        compiler_params=params(24),
        cost_estimate=cost(2 * ROWS * COLS * NPROJ, 2 * (2 * ROWS + NPROJ) * COLS),
        name="finish",
    )(place, coupled, gvec, in_vmem(wave), in_hbm(whole_own), whole_other)


def band_perm(move):
    pairs = []
    for b in range(N_BAND):
        x, y, c = move(b // 8, (b // 2) % 4, b % 2)
        pairs.append((b, (x % 2) * 8 + (y % 4) * 2 + c))
    return pairs


def along_band(value, move):
    return lax.ppermute(value, "band", band_perm(move))


def swap(value):
    return along_band(value, lambda x, y, c: (x, y, 1 - c))


def ring(value):
    return along_band(value, lambda x, y, c: (x, y + 1 - 2 * c, c))


def against_ring(value):
    return along_band(value, lambda x, y, c: (x, y - 1 + 2 * c, c))


def to_other_x(value):
    return along_band(value, lambda x, y, c: (x + 1, y, c))


def near_exchange(value):
    groups = [[zh * NEAR + n for n in range(NEAR)] for zh in range(N_Z_HI)]
    return lax.all_to_all(value, "coef", 0, 0, axis_index_groups=groups, tiled=True)


def far_exchange(value):
    groups = [
        [(zh * NEAR + n) * N_BAND + chip * 2 + core for zh in range(N_Z_HI) for core in range(2)]
        for n in range(NEAR) for chip in range(N_BAND // 2)
    ]
    return lax.all_to_all(value, ("coef", "band"), 0, 0, axis_index_groups=groups, tiled=True)


def on_device(wave, projector, gvec, atom_of, dion, qaug):
    b, c = lax.axis_index("band"), lax.axis_index("coef")
    x, y, core, z_hi = b >> 3, (b >> 1) & 3, b & 1, c >> 3
    order = [y, (y + 3 + 2 * core) & 3, (y + 1 + 2 * core) & 3, (y + 2) & 3]
    place = jnp.stack(
        [core, z_hi] + [x * 4 + at for at in order] + [(1 - x) * 4 + at for at in order]).astype(jnp.int32)

    across = to_other_x(projector)
    before, after = ring(projector), against_ring(projector)
    far = ring(before)
    stat, wave_v = stats(wave, gvec)
    across, after, far, own_wave, stat = lax.optimization_barrier((across, after, far, wave, stat))
    far_x = to_other_x(far)
    before_x, after_x = ring(across), against_ring(across)
    wave_other = swap(own_wave)
    shards = [projector, before, after, far, across, before_x, after_x, far_x]
    message, whole = intersect(place, stat, wave_v, wave_other, shards)
    message, dion = lax.optimization_barrier((message, dion))
    weights = masked_weights(atom_of, dion, qaug)

    received, weights = lax.optimization_barrier((near_exchange(message), weights))
    keep, message = near_sum(place, received)
    coupled = near_exchange(couple(place, keep, far_exchange(message), weights))
    return finish(place, coupled, wave_v, gvec, whole, swap(whole))


def solution(mesh):
    in_specs = (P("band", "coef"), P("band", "coef"), P(None, "coef"), P(), P(), P())
    out_specs = P("band", "coef")
    return jax.shard_map(
        on_device, mesh=mesh, in_specs=in_specs, out_specs=out_specs, check_vma=False
    )
```

```python
import functools
import jax
import jax.numpy as jnp
from jax import lax
from jax.experimental import pallas as pl
from jax.experimental.pallas import tpu as pltpu
from jax.sharding import PartitionSpec as P

kinetic_unit = 0.005
f32 = jnp.float32
bf16 = jnp.bfloat16

N_COEF = 32
N_BAND = 16
ROWS = 256
COLS = 4096
NPROJ = 512
SHARD = NPROJ // N_BAND
HALF_PROJ = NPROJ // 2
QUARTER_PROJ = NPROJ // 4
NEAR = 8
BANDS = ROWS // NEAR
STAT_ROWS = BANDS // 4
NEAR_ROWS = 2 * BANDS + STAT_ROWS
FAR_ROWS = BANDS + STAT_ROWS
N_Z_HI = N_COEF // NEAR
FAR = 2 * N_Z_HI

anywhere = pl.BlockSpec(memory_space=pl.ANY)
vmem = pl.BlockSpec(memory_space=pltpu.VMEM)
smem = pl.BlockSpec(memory_space=pltpu.SMEM)

CORE, Z_HI, ORDER = 0, 1, 2


def in_vmem(value):
    return pltpu.with_memory_space_constraint(value, pltpu.VMEM)


def in_hbm(value):
    return pltpu.with_memory_space_constraint(value, pltpu.HBM)


def params(mib):
    return pltpu.CompilerParams(vmem_limit_bytes=mib * 1024 * 1024)


def cost(flops, bytes_accessed):
    return pl.CostEstimate(flops=flops, bytes_accessed=bytes_accessed, transcendentals=0)


def pieces(value):
    hi = value.astype(bf16).astype(f32)
    rest = value - hi
    mid = rest.astype(bf16).astype(f32)
    lo = (rest - mid).astype(bf16).astype(f32)
    return hi, mid, lo


def stat_lanes():
    return lax.broadcasted_iota(jnp.int32, (STAT_ROWS, HALF_PROJ), 1)


def split_rows(value):
    lane = stat_lanes() & 63
    hi, mid, lo = [jnp.where((lane == 0) | (lane == 3), piece, 0.0) for piece in pieces(value)]
    return hi + pltpu.roll(mid, 1, 1) + pltpu.roll(lo, 2, 1)


def join_rows(packed):
    return packed + pltpu.roll(packed, HALF_PROJ - 1, 1) + pltpu.roll(packed, HALF_PROJ - 2, 1)


def to_rows(first, second):
    lane = stat_lanes()
    out = jnp.zeros((STAT_ROWS, HALF_PROJ), f32)
    for k in range(4):
        rows = slice(k * STAT_ROWS, (k + 1) * STAT_ROWS)
        out = jnp.where(lane == 64 * k, first[rows], jnp.where(lane == 64 * k + 3, second[rows], out))
    return split_rows(out)


def from_rows(packed):
    lane = stat_lanes()
    columns = []
    for begin in (0, 3):
        columns.append(jnp.concatenate([
            jnp.sum(jnp.where((lane >= 64 * k + begin) & (lane < 64 * k + begin + 3), packed, 0.0), axis=1, keepdims=True)
            for k in range(4)
        ], axis=0))
    return columns


def kinetic(gvec):
    comps = gvec.astype(f32)
    return kinetic_unit * (comps[0:1] * comps[0:1] + comps[1:2] * comps[1:2] + comps[2:3] * comps[2:3])


def stats_kernel(wave, gvec, stat, wave_v, sems):
    copies = [
        pltpu.make_async_copy(
            wave.at[pl.ds(n * BANDS, BANDS), :], wave_v.at[pl.ds(n * BANDS, BANDS), :], sems.at[n])
        for n in range(NEAR)
    ]
    for copy in copies:
        copy.start()
    kin = kinetic(gvec[...])
    for n, copy in enumerate(copies):
        copy.wait()
        value = wave_v[n * BANDS:(n + 1) * BANDS, :].astype(f32)
        square = value * value
        sq = jnp.sum(square, axis=1, keepdims=True)
        ksq = jnp.sum(square * kin, axis=1, keepdims=True)
        stat[n * STAT_ROWS:(n + 1) * STAT_ROWS, :] = to_rows(sq, ksq)


def stats(wave, gvec):
    return pl.pallas_call(
        stats_kernel,
        in_specs=[anywhere, vmem],
        out_specs=[vmem, vmem],
        out_shape=[
            jax.ShapeDtypeStruct((NEAR * STAT_ROWS, HALF_PROJ), f32),
            pltpu.VMEM((ROWS, COLS), bf16),
        ],
        scratch_shapes=[pltpu.SemaphoreType.DMA((NEAR,))],
        compiler_params=params(16),
        cost_estimate=cost(5 * ROWS * COLS, 2 * ROWS * COLS),
        name="stats",
    )(in_hbm(wave), gvec)


def weights_kernel(atom_of, dion, qaug, out):
    number = lax.broadcasted_iota(jnp.int32, (64, NPROJ), 0)
    member = jnp.where(atom_of[...] == number, 1.0, 0.0).astype(bf16)
    same = lax.dot_general(member, member, (((0,), (0,)), ((), ())), preferred_element_type=f32) > 0.5
    to = lax.broadcasted_iota(jnp.int32, (NPROJ, NPROJ), 0)
    source = ((to & 0xE0) << 1) | ((to >> 8) << 5) | (to & 31)
    order = jnp.where(source == lax.broadcasted_iota(jnp.int32, (NPROJ, NPROJ), 1), 1.0, 0.0).astype(bf16)
    for at, matrix in enumerate((dion, qaug)):
        value = jnp.where(same, matrix[...].astype(f32), 0.0).astype(bf16)
        rows = jnp.dot(order, value, preferred_element_type=f32).astype(bf16)
        out[:, at * NPROJ:(at + 1) * NPROJ] = lax.dot_general(
            rows, order, (((1,), (1,)), ((), ())), preferred_element_type=f32).astype(bf16)


def masked_weights(atom_of, dion, qaug):
    return pl.pallas_call(
        weights_kernel,
        in_specs=[vmem] * 3,
        out_specs=vmem,
        out_shape=jax.ShapeDtypeStruct((NPROJ, 2 * NPROJ), bf16),
        compiler_params=params(24),
        cost_estimate=cost(9 * NPROJ ** 3, 8 * NPROJ * NPROJ),
        name="masked_weights",
    )(atom_of.reshape(1, NPROJ), in_hbm(dion), in_hbm(qaug))


def against(left, right):
    return lax.dot_general(left, right, (((1,), (1,)), ((), ())), preferred_element_type=f32)


N_SHARDS = HALF_PROJ // SHARD


def intersect_kernel(place, stat, wave_own, wave_other, *refs):
    shards = refs[:N_SHARDS]
    message, whole, whole_v, message_v, out_sem = refs[N_SHARDS:]
    for i, shard in enumerate(shards):
        at = pl.multiple_of(place[ORDER + i] * SHARD, SHARD)
        whole_v[pl.ds(at, SHARD), :] = shard[...]
    back = pltpu.make_async_copy(whole_v, whole, out_sem)
    back.start()
    for core, wave in enumerate((wave_own, wave_other)):
        total = against(wave[...], whole_v[...])
        for n in range(NEAR):
            at = n * NEAR_ROWS + core * BANDS
            message_v[at:at + BANDS, :] = total[n * BANDS:(n + 1) * BANDS]
    for n in range(NEAR):
        at = n * NEAR_ROWS + 2 * BANDS
        message_v[at:at + STAT_ROWS, :] = stat[n * STAT_ROWS:(n + 1) * STAT_ROWS, :]
    message[...] = message_v[...].astype(bf16)
    back.wait()


def intersect(place, stat, wave_own, wave_other, shards):
    return pl.pallas_call(
        intersect_kernel,
        in_specs=[smem] + [vmem] * (3 + N_SHARDS),
        out_specs=[vmem, anywhere],
        out_shape=[
            jax.ShapeDtypeStruct((NEAR * NEAR_ROWS, HALF_PROJ), bf16),
            pltpu.HBM((HALF_PROJ, COLS), bf16),
        ],
        scratch_shapes=[
            pltpu.VMEM((HALF_PROJ, COLS), bf16),
            pltpu.VMEM((NEAR * NEAR_ROWS, HALF_PROJ), f32),
            pltpu.SemaphoreType.DMA,
        ],
        compiler_params=params(24),
        cost_estimate=cost(4 * ROWS * COLS * HALF_PROJ, 2 * (2 * ROWS + 2 * HALF_PROJ) * COLS),
        name="intersect",
    )(place, stat, in_vmem(wave_own), in_vmem(wave_other), *[in_vmem(shard) for shard in shards])


def near_sum_kernel(place, received, keep, message, message_v):
    total = jnp.sum(received[...].astype(f32).reshape(NEAR, NEAR_ROWS, HALF_PROJ), axis=0)
    keep[...] = total[:BANDS]
    rows = split_rows(join_rows(total[2 * BANDS:]))
    core = place[CORE]
    for zh in range(N_Z_HI):
        for c, value in ((core, total[:BANDS]), (1 - core, total[BANDS:2 * BANDS])):
            at = pl.multiple_of((zh * 2 + c) * FAR_ROWS, STAT_ROWS)
            message_v[pl.ds(at, BANDS), :] = value
            message_v[pl.ds(at + BANDS, STAT_ROWS), :] = rows
    message[...] = message_v[...].astype(bf16)


def near_sum(place, received):
    return pl.pallas_call(
        near_sum_kernel,
        in_specs=[smem, vmem],
        out_specs=[vmem, vmem],
        out_shape=[
            jax.ShapeDtypeStruct((BANDS, HALF_PROJ), f32),
            jax.ShapeDtypeStruct((FAR * FAR_ROWS, HALF_PROJ), bf16),
        ],
        scratch_shapes=[pltpu.VMEM((FAR * FAR_ROWS, HALF_PROJ), f32)],
        compiler_params=params(16),
        cost_estimate=cost(NEAR * NEAR_ROWS * HALF_PROJ, 3 * NEAR * NEAR_ROWS * HALF_PROJ),
        name="near_sum",
    )(place, received)


def couple_kernel(place, keep, received, weights, out):
    blocks = received[...].astype(f32).reshape(FAR, FAR_ROWS, HALF_PROJ)
    core = place[CORE]
    own_at = place[Z_HI] * 2 + core
    halves, packed = [], []
    for c in range(2):
        total = jnp.zeros((BANDS, HALF_PROJ), f32)
        rows = jnp.zeros((STAT_ROWS, HALF_PROJ), f32)
        for zh in range(N_Z_HI):
            block = blocks[zh * 2 + c]
            total += jnp.where(own_at == zh * 2 + c, keep[...], block[:BANDS])
            rows += block[BANDS:]
        halves.append(total)
        packed.append(rows)
    inter = jnp.concatenate(halves, axis=1)
    sq, ksq = from_rows(jnp.where(core == 0, packed[0], packed[1]))
    stacked = jnp.concatenate(pieces(inter), axis=0).astype(bf16)
    both = jnp.dot(stacked, weights[...], preferred_element_type=f32)
    both = both[:BANDS] + (both[BANDS:2 * BANDS] + both[2 * BANDS:])
    pd, pq = both[:, :NPROJ], both[:, NPROJ:]
    energy = (ksq + jnp.sum(inter * pd, axis=1, keepdims=True)) / (
        sq + jnp.sum(inter * pq, axis=1, keepdims=True))
    ekin = ksq / (sq + 1e-6)
    coupled = pd - energy * pq
    block = jnp.concatenate([coupled[:, :HALF_PROJ], coupled[:, HALF_PROJ:], to_rows(energy, ekin)], axis=0)
    out[...] = jnp.concatenate([block] * NEAR, axis=0).astype(bf16)


def couple(place, keep, received, weights):
    return pl.pallas_call(
        couple_kernel,
        in_specs=[smem] + [vmem] * 3,
        out_specs=vmem,
        out_shape=jax.ShapeDtypeStruct((NEAR * NEAR_ROWS, HALF_PROJ), bf16),
        compiler_params=params(16),
        cost_estimate=cost(12 * BANDS * NPROJ * NPROJ, 4 * NPROJ * NPROJ + 4 * ROWS * NPROJ),
        name="couple",
    )(place, keep, received, weights)


TILE = 512
N_TILES = COLS // TILE
CHUNK = 16


def finish_kernel(place, coupled, gvec, wave, whole_own, whole_other, out,
                  whole_v, out_v, halves_v, energy_v, scale_v, even_v, odd_v, sems, out_sems):
    def columns(tile):
        return pl.ds(pl.multiple_of(tile * TILE, TILE), TILE)

    def copies(tile):
        cols = columns(tile)
        return [
            pltpu.make_async_copy(
                source.at[:, cols], whole_v.at[pl.ds(i * HALF_PROJ, HALF_PROJ), cols], sems.at[tile, i])
            for i, source in enumerate((whole_own, whole_other))
        ]

    def out_copy(tile):
        cols = columns(tile)
        return pltpu.make_async_copy(out_v.at[:, cols], out.at[:, cols], out_sems.at[tile])

    def arrive(tile):
        for copy in copies(tile):
            copy.wait()

    def expand(tile, expanded_v):
        cols = columns(tile)
        expanded_v[...] = jnp.dot(halves_v[...], whole_v[:, cols], preferred_element_type=f32)

    def conclude(tile, expanded_v):
        cols = columns(tile)
        kin = jnp.broadcast_to(kinetic(gvec[:, cols]), (CHUNK, TILE))
        for i in range(ROWS // CHUNK):
            rows = slice(i * CHUNK, (i + 1) * CHUNK)
            energy = jnp.concatenate([energy_v[rows, :]] * (TILE // 128), axis=1)
            scale = jnp.concatenate([scale_v[rows, :]] * (TILE // 128), axis=1)
            resid = (kin - energy) * wave[rows, cols].astype(f32) + expanded_v[rows, :]
            u = kin * scale
            v = u * u
            num = (1.0 + u) * (1.0 + v)
            inverse = pl.reciprocal(num + 3.0 * (v * v), approx=True)
            out_v[rows, cols] = ((num * inverse) * resid).astype(bf16)

    for tile in range(N_TILES):
        for copy in copies(tile):
            copy.start()
    core = place[CORE]
    blocks = coupled[...].astype(f32).reshape(NEAR, NEAR_ROWS, HALF_PROJ)
    for n in range(NEAR):
        rows = slice(n * BANDS, (n + 1) * BANDS)
        first, second = blocks[n, :BANDS].astype(bf16), blocks[n, BANDS:2 * BANDS].astype(bf16)
        halves_v[rows, :HALF_PROJ] = jnp.where(core == 0, first, second)
        halves_v[rows, HALF_PROJ:] = jnp.where(core == 0, second, first)
        energy, ekin = from_rows(blocks[n, 2 * BANDS:])
        energy_v[rows, :] = jnp.broadcast_to(energy, (BANDS, 128))
        scale_v[rows, :] = jnp.broadcast_to((2.0 / 3.0) / ekin, (BANDS, 128))
    arrive(0)
    expand(0, even_v)

    @pl.loop(0, N_TILES // 2)
    def _(i):
        arrive(2 * i + 1)

        @pl.when(i + 1 < N_TILES // 2)
        def _():
            arrive(2 * i + 2)

        expand(2 * i + 1, odd_v)
        conclude(2 * i, even_v)
        out_copy(2 * i).start()
        expand(jnp.minimum(2 * i + 2, N_TILES - 1), even_v)
        conclude(2 * i + 1, odd_v)
        out_copy(2 * i + 1).start()

    for tile in range(N_TILES):
        out_copy(tile).wait()


def finish(place, coupled, wave, gvec, whole_own, whole_other):
    return pl.pallas_call(
        finish_kernel,
        in_specs=[smem] + [vmem] * 3 + [anywhere] * 2,
        out_specs=anywhere,
        out_shape=jax.ShapeDtypeStruct((ROWS, COLS), bf16),
        scratch_shapes=[pltpu.VMEM((NPROJ, COLS), bf16), pltpu.VMEM((ROWS, COLS), bf16), pltpu.VMEM((ROWS, NPROJ), bf16)]
        + [pltpu.VMEM((ROWS, 128), f32)] * 2 + [pltpu.VMEM((ROWS, TILE), f32)] * 2
        + [pltpu.SemaphoreType.DMA((N_TILES, 2)), pltpu.SemaphoreType.DMA((N_TILES,))],
        compiler_params=params(24),
        cost_estimate=cost(2 * ROWS * COLS * NPROJ, 2 * (2 * ROWS + NPROJ) * COLS),
        name="finish",
    )(place, coupled, gvec, in_vmem(wave), in_hbm(whole_own), whole_other)


def band_perm(move):
    pairs = []
    for b in range(N_BAND):
        x, y, c = move(b // 8, (b // 2) % 4, b % 2)
        pairs.append((b, (x % 2) * 8 + (y % 4) * 2 + c))
    return pairs


def along_band(value, move):
    return lax.ppermute(value, "band", band_perm(move))


def swap(value):
    return along_band(value, lambda x, y, c: (x, y, 1 - c))


def ring(value):
    return along_band(value, lambda x, y, c: (x, y + 1 - 2 * c, c))


def against_ring(value):
    return along_band(value, lambda x, y, c: (x, y - 1 + 2 * c, c))


def to_other_x(value):
    return along_band(value, lambda x, y, c: (x + 1, y, c))


def near_exchange(value):
    groups = [[zh * NEAR + n for n in range(NEAR)] for zh in range(N_Z_HI)]
    return lax.all_to_all(value, "coef", 0, 0, axis_index_groups=groups, tiled=True)


def far_exchange(value):
    groups = [
        [(zh * NEAR + n) * N_BAND + chip * 2 + core for zh in range(N_Z_HI) for core in range(2)]
        for n in range(NEAR) for chip in range(N_BAND // 2)
    ]
    return lax.all_to_all(value, ("coef", "band"), 0, 0, axis_index_groups=groups, tiled=True)


def on_device(wave, projector, gvec, atom_of, dion, qaug):
    b, c = lax.axis_index("band"), lax.axis_index("coef")
    x, y, core, z_hi = b >> 3, (b >> 1) & 3, b & 1, c >> 3
    order = [y, (y + 3 + 2 * core) & 3, (y + 1 + 2 * core) & 3, (y + 2) & 3]
    place = jnp.stack(
        [core, z_hi] + [x * 4 + at for at in order] + [(1 - x) * 4 + at for at in order]).astype(jnp.int32)

    across = to_other_x(projector)
    before, after = ring(projector), against_ring(projector)
    far = ring(before)
    stat, wave_v = stats(wave, gvec)
    across, after, far, own_wave, stat, late_dion = lax.optimization_barrier((across, after, far, wave, stat, dion))
    far_x = to_other_x(far)
    before_x, after_x = ring(across), against_ring(across)
    wave_other = swap(own_wave)
    shards = [projector, before, after, far, across, before_x, after_x, far_x]
    weights = masked_weights(atom_of, late_dion, qaug)
    stat, weights = lax.optimization_barrier((stat, weights))
    message, whole = intersect(place, stat, wave_v, wave_other, shards)

    keep, message = near_sum(place, near_exchange(message))
    coupled = near_exchange(couple(place, keep, far_exchange(message), weights))
    return finish(place, coupled, wave_v, gvec, whole, swap(whole))


def solution(mesh):
    in_specs = (P("band", "coef"), P("band", "coef"), P(None, "coef"), P(), P(), P())
    out_specs = P("band", "coef")
    return jax.shard_map(
        on_device, mesh=mesh, in_specs=in_specs, out_specs=out_specs, check_vma=False
    )
```

```python
import functools
import jax
import jax.numpy as jnp
from jax import lax
from jax.experimental import pallas as pl
from jax.experimental.pallas import tpu as pltpu
from jax.sharding import PartitionSpec as P

kinetic_unit = 0.005
f32 = jnp.float32
bf16 = jnp.bfloat16

N_COEF = 32
N_BAND = 16
ROWS = 256
COLS = 4096
NPROJ = 512
SHARD = NPROJ // N_BAND
HALF_PROJ = NPROJ // 2
QUARTER_PROJ = NPROJ // 4
NEAR = 8
BANDS = ROWS // NEAR
STAT_ROWS = BANDS // 4
NEAR_ROWS = 2 * BANDS + STAT_ROWS
FAR_ROWS = BANDS + STAT_ROWS
N_Z_HI = N_COEF // NEAR
FAR = 2 * N_Z_HI

anywhere = pl.BlockSpec(memory_space=pl.ANY)
vmem = pl.BlockSpec(memory_space=pltpu.VMEM)
smem = pl.BlockSpec(memory_space=pltpu.SMEM)

CORE, Z_HI, ORDER = 0, 1, 2


def in_vmem(value):
    return pltpu.with_memory_space_constraint(value, pltpu.VMEM)


def in_hbm(value):
    return pltpu.with_memory_space_constraint(value, pltpu.HBM)


def params(mib):
    return pltpu.CompilerParams(vmem_limit_bytes=mib * 1024 * 1024)


def cost(flops, bytes_accessed):
    return pl.CostEstimate(flops=flops, bytes_accessed=bytes_accessed, transcendentals=0)


def pieces(value):
    hi = value.astype(bf16).astype(f32)
    rest = value - hi
    mid = rest.astype(bf16).astype(f32)
    lo = (rest - mid).astype(bf16).astype(f32)
    return hi, mid, lo


def stat_lanes():
    return lax.broadcasted_iota(jnp.int32, (STAT_ROWS, HALF_PROJ), 1)


def split_rows(value):
    lane = stat_lanes() & 63
    hi, mid, lo = [jnp.where((lane == 0) | (lane == 3), piece, 0.0) for piece in pieces(value)]
    return hi + pltpu.roll(mid, 1, 1) + pltpu.roll(lo, 2, 1)


def join_rows(packed):
    return packed + pltpu.roll(packed, HALF_PROJ - 1, 1) + pltpu.roll(packed, HALF_PROJ - 2, 1)


def to_rows(first, second):
    lane = stat_lanes()
    out = jnp.zeros((STAT_ROWS, HALF_PROJ), f32)
    for k in range(4):
        rows = slice(k * STAT_ROWS, (k + 1) * STAT_ROWS)
        out = jnp.where(lane == 64 * k, first[rows], jnp.where(lane == 64 * k + 3, second[rows], out))
    return split_rows(out)


def from_rows(packed):
    lane = stat_lanes()
    columns = []
    for begin in (0, 3):
        columns.append(jnp.concatenate([
            jnp.sum(jnp.where((lane >= 64 * k + begin) & (lane < 64 * k + begin + 3), packed, 0.0), axis=1, keepdims=True)
            for k in range(4)
        ], axis=0))
    return columns


def kinetic(gvec):
    comps = gvec.astype(f32)
    return kinetic_unit * (comps[0:1] * comps[0:1] + comps[1:2] * comps[1:2] + comps[2:3] * comps[2:3])


def stats_kernel(wave, gvec, stat, wave_v, sems):
    copies = [
        pltpu.make_async_copy(
            wave.at[pl.ds(n * BANDS, BANDS), :], wave_v.at[pl.ds(n * BANDS, BANDS), :], sems.at[n])
        for n in range(NEAR)
    ]
    for copy in copies:
        copy.start()
    kin = kinetic(gvec[...])
    for n, copy in enumerate(copies):
        copy.wait()
        value = wave_v[n * BANDS:(n + 1) * BANDS, :].astype(f32)
        square = value * value
        sq = jnp.sum(square, axis=1, keepdims=True)
        ksq = jnp.sum(square * kin, axis=1, keepdims=True)
        stat[n * STAT_ROWS:(n + 1) * STAT_ROWS, :] = to_rows(sq, ksq)


def stats(wave, gvec):
    return pl.pallas_call(
        stats_kernel,
        in_specs=[anywhere, vmem],
        out_specs=[vmem, vmem],
        out_shape=[
            jax.ShapeDtypeStruct((NEAR * STAT_ROWS, HALF_PROJ), f32),
            pltpu.VMEM((ROWS, COLS), bf16),
        ],
        scratch_shapes=[pltpu.SemaphoreType.DMA((NEAR,))],
        compiler_params=params(16),
        cost_estimate=cost(5 * ROWS * COLS, 2 * ROWS * COLS),
        name="stats",
    )(in_hbm(wave), gvec)


def weights_kernel(atom_of, dion, qaug, out):
    number = lax.broadcasted_iota(jnp.int32, (64, NPROJ), 0)
    member = jnp.where(atom_of[...] == number, 1.0, 0.0).astype(bf16)
    same = lax.dot_general(member, member, (((0,), (0,)), ((), ())), preferred_element_type=f32) > 0.5
    to = lax.broadcasted_iota(jnp.int32, (NPROJ, NPROJ), 0)
    source = ((to & 0xE0) << 1) | ((to >> 8) << 5) | (to & 31)
    order = jnp.where(source == lax.broadcasted_iota(jnp.int32, (NPROJ, NPROJ), 1), 1.0, 0.0).astype(bf16)
    for at, matrix in enumerate((dion, qaug)):
        value = jnp.where(same, matrix[...].astype(f32), 0.0).astype(bf16)
        rows = jnp.dot(order, value, preferred_element_type=f32).astype(bf16)
        out[:, at * NPROJ:(at + 1) * NPROJ] = lax.dot_general(
            rows, order, (((1,), (1,)), ((), ())), preferred_element_type=f32).astype(bf16)


def masked_weights(atom_of, dion, qaug):
    return pl.pallas_call(
        weights_kernel,
        in_specs=[vmem] * 3,
        out_specs=vmem,
        out_shape=jax.ShapeDtypeStruct((NPROJ, 2 * NPROJ), bf16),
        compiler_params=params(24),
        cost_estimate=cost(9 * NPROJ ** 3, 8 * NPROJ * NPROJ),
        name="masked_weights",
    )(atom_of.reshape(1, NPROJ), in_hbm(dion), in_hbm(qaug))


def against(left, right):
    return lax.dot_general(left, right, (((1,), (1,)), ((), ())), preferred_element_type=f32)


N_SHARDS = HALF_PROJ // SHARD


def intersect_kernel(place, stat, wave_own, wave_other, *refs):
    shards = refs[:N_SHARDS]
    message, whole, whole_v, message_v, out_sem = refs[N_SHARDS:]
    for i, shard in enumerate(shards):
        at = pl.multiple_of(place[ORDER + i] * SHARD, SHARD)
        whole_v[pl.ds(at, SHARD), :] = shard[...]
    back = pltpu.make_async_copy(whole_v, whole, out_sem)
    back.start()
    for core, wave in enumerate((wave_own, wave_other)):
        total = against(wave[...], whole_v[...])
        for n in range(NEAR):
            at = n * NEAR_ROWS + core * BANDS
            message_v[at:at + BANDS, :] = total[n * BANDS:(n + 1) * BANDS]
    for n in range(NEAR):
        at = n * NEAR_ROWS + 2 * BANDS
        message_v[at:at + STAT_ROWS, :] = stat[n * STAT_ROWS:(n + 1) * STAT_ROWS, :]
    message[...] = message_v[...].astype(bf16)
    back.wait()


def intersect(place, stat, wave_own, wave_other, shards):
    return pl.pallas_call(
        intersect_kernel,
        in_specs=[smem] + [vmem] * (3 + N_SHARDS),
        out_specs=[vmem, anywhere],
        out_shape=[
            jax.ShapeDtypeStruct((NEAR * NEAR_ROWS, HALF_PROJ), bf16),
            pltpu.HBM((HALF_PROJ, COLS), bf16),
        ],
        scratch_shapes=[
            pltpu.VMEM((HALF_PROJ, COLS), bf16),
            pltpu.VMEM((NEAR * NEAR_ROWS, HALF_PROJ), f32),
            pltpu.SemaphoreType.DMA,
        ],
        compiler_params=params(24),
        cost_estimate=cost(4 * ROWS * COLS * HALF_PROJ, 2 * (2 * ROWS + 2 * HALF_PROJ) * COLS),
        name="intersect",
    )(place, stat, in_vmem(wave_own), in_vmem(wave_other), *[in_vmem(shard) for shard in shards])


def near_sum_kernel(place, received, keep, message, message_v):
    total = jnp.sum(received[...].astype(f32).reshape(NEAR, NEAR_ROWS, HALF_PROJ), axis=0)
    keep[...] = total[:BANDS]
    rows = split_rows(join_rows(total[2 * BANDS:]))
    core = place[CORE]
    for zh in range(N_Z_HI):
        for c, value in ((core, total[:BANDS]), (1 - core, total[BANDS:2 * BANDS])):
            at = pl.multiple_of((zh * 2 + c) * FAR_ROWS, STAT_ROWS)
            message_v[pl.ds(at, BANDS), :] = value
            message_v[pl.ds(at + BANDS, STAT_ROWS), :] = rows
    message[...] = message_v[...].astype(bf16)


def near_sum(place, received):
    return pl.pallas_call(
        near_sum_kernel,
        in_specs=[smem, vmem],
        out_specs=[vmem, vmem],
        out_shape=[
            jax.ShapeDtypeStruct((BANDS, HALF_PROJ), f32),
            jax.ShapeDtypeStruct((FAR * FAR_ROWS, HALF_PROJ), bf16),
        ],
        scratch_shapes=[pltpu.VMEM((FAR * FAR_ROWS, HALF_PROJ), f32)],
        compiler_params=params(16),
        cost_estimate=cost(NEAR * NEAR_ROWS * HALF_PROJ, 3 * NEAR * NEAR_ROWS * HALF_PROJ),
        name="near_sum",
    )(place, received)


def couple_kernel(place, keep, received, weights, out):
    blocks = received[...].astype(f32).reshape(FAR, FAR_ROWS, HALF_PROJ)
    core = place[CORE]
    own_at = place[Z_HI] * 2 + core
    halves, packed = [], []
    for c in range(2):
        total = jnp.zeros((BANDS, HALF_PROJ), f32)
        rows = jnp.zeros((STAT_ROWS, HALF_PROJ), f32)
        for zh in range(N_Z_HI):
            block = blocks[zh * 2 + c]
            total += jnp.where(own_at == zh * 2 + c, keep[...], block[:BANDS])
            rows += block[BANDS:]
        halves.append(total)
        packed.append(rows)
    inter = jnp.concatenate(halves, axis=1)
    sq, ksq = from_rows(jnp.where(core == 0, packed[0], packed[1]))
    stacked = jnp.concatenate(pieces(inter), axis=0).astype(bf16)
    both = jnp.dot(stacked, weights[...], preferred_element_type=f32)
    both = both[:BANDS] + (both[BANDS:2 * BANDS] + both[2 * BANDS:])
    pd, pq = both[:, :NPROJ], both[:, NPROJ:]
    energy = (ksq + jnp.sum(inter * pd, axis=1, keepdims=True)) / (
        sq + jnp.sum(inter * pq, axis=1, keepdims=True))
    ekin = ksq / (sq + 1e-6)
    coupled = pd - energy * pq
    block = jnp.concatenate([coupled[:, :HALF_PROJ], coupled[:, HALF_PROJ:], to_rows(energy, ekin)], axis=0)
    out[...] = jnp.concatenate([block] * NEAR, axis=0).astype(bf16)


def couple(place, keep, received, weights):
    return pl.pallas_call(
        couple_kernel,
        in_specs=[smem] + [vmem] * 3,
        out_specs=vmem,
        out_shape=jax.ShapeDtypeStruct((NEAR * NEAR_ROWS, HALF_PROJ), bf16),
        compiler_params=params(16),
        cost_estimate=cost(12 * BANDS * NPROJ * NPROJ, 4 * NPROJ * NPROJ + 4 * ROWS * NPROJ),
        name="couple",
    )(place, keep, received, weights)


TILE = 512
N_TILES = COLS // TILE
CHUNK = 16


def finish_kernel(place, coupled, gvec, wave, whole_own, whole_other, out,
                  whole_v, out_v, halves_v, energy_v, scale_v, even_v, odd_v, sems, out_sems):
    def columns(tile):
        return pl.ds(pl.multiple_of(tile * TILE, TILE), TILE)

    def copies(tile):
        cols = columns(tile)
        return [
            pltpu.make_async_copy(
                source.at[:, cols], whole_v.at[pl.ds(i * HALF_PROJ, HALF_PROJ), cols], sems.at[tile, i])
            for i, source in enumerate((whole_own, whole_other))
        ]

    def out_copy(tile):
        cols = columns(tile)
        return pltpu.make_async_copy(out_v.at[:, cols], out.at[:, cols], out_sems.at[tile])

    def arrive(tile):
        for copy in copies(tile):
            copy.wait()

    def expand(tile, expanded_v):
        cols = columns(tile)
        expanded_v[...] = jnp.dot(halves_v[...], whole_v[:, cols], preferred_element_type=f32)

    def conclude(tile, expanded_v):
        cols = columns(tile)
        kin = jnp.broadcast_to(kinetic(gvec[:, cols]), (CHUNK, TILE))
        for i in range(ROWS // CHUNK):
            rows = slice(i * CHUNK, (i + 1) * CHUNK)
            energy = jnp.concatenate([energy_v[rows, :]] * (TILE // 128), axis=1)
            scale = jnp.concatenate([scale_v[rows, :]] * (TILE // 128), axis=1)
            resid = (kin - energy) * wave[rows, cols].astype(f32) + expanded_v[rows, :]
            t = kin * scale
            square = t * t
            num = (3.0 + t) * (9.0 + square)
            inverse = pl.reciprocal(num + square * square, approx=True)
            out_v[rows, cols] = ((num * inverse) * resid).astype(bf16)

    def depart(tiles):
        for tile in tiles:
            for copy in copies(tile):
                copy.start()

    depart(range(3))
    core = place[CORE]
    blocks = coupled[...].astype(f32).reshape(NEAR, NEAR_ROWS, HALF_PROJ)
    for n in range(NEAR):
        rows = slice(n * BANDS, (n + 1) * BANDS)
        first, second = blocks[n, :BANDS].astype(bf16), blocks[n, BANDS:2 * BANDS].astype(bf16)
        halves_v[rows, :HALF_PROJ] = jnp.where(core == 0, first, second)
        halves_v[rows, HALF_PROJ:] = jnp.where(core == 0, second, first)
        energy, ekin = from_rows(blocks[n, 2 * BANDS:])
        energy_v[rows, :] = jnp.broadcast_to(energy, (BANDS, 128))
        scale_v[rows, :] = jnp.broadcast_to(2.0 / ekin, (BANDS, 128))
    depart(range(3, N_TILES))
    arrive(0)
    expand(0, even_v)

    @pl.loop(0, N_TILES // 2)
    def _(i):
        arrive(2 * i + 1)

        @pl.when(i + 1 < N_TILES // 2)
        def _():
            arrive(2 * i + 2)

        expand(2 * i + 1, odd_v)
        conclude(2 * i, even_v)
        out_copy(2 * i).start()
        expand(jnp.minimum(2 * i + 2, N_TILES - 1), even_v)
        conclude(2 * i + 1, odd_v)
        out_copy(2 * i + 1).start()

    for tile in range(N_TILES):
        out_copy(tile).wait()


def finish(place, coupled, wave, gvec, whole_own, whole_other):
    return pl.pallas_call(
        finish_kernel,
        in_specs=[smem] + [vmem] * 3 + [anywhere] * 2,
        out_specs=anywhere,
        out_shape=jax.ShapeDtypeStruct((ROWS, COLS), bf16),
        scratch_shapes=[pltpu.VMEM((NPROJ, COLS), bf16), pltpu.VMEM((ROWS, COLS), bf16), pltpu.VMEM((ROWS, NPROJ), bf16)]
        + [pltpu.VMEM((ROWS, 128), f32)] * 2 + [pltpu.VMEM((ROWS, TILE), f32)] * 2
        + [pltpu.SemaphoreType.DMA((N_TILES, 2)), pltpu.SemaphoreType.DMA((N_TILES,))],
        compiler_params=params(24),
        cost_estimate=cost(2 * ROWS * COLS * NPROJ, 2 * (2 * ROWS + NPROJ) * COLS),
        name="finish",
    )(place, coupled, gvec, in_vmem(wave), in_hbm(whole_own), whole_other)


def band_perm(move):
    pairs = []
    for b in range(N_BAND):
        x, y, c = move(b // 8, (b // 2) % 4, b % 2)
        pairs.append((b, (x % 2) * 8 + (y % 4) * 2 + c))
    return pairs


def along_band(value, move):
    return lax.ppermute(value, "band", band_perm(move))


def swap(value):
    return along_band(value, lambda x, y, c: (x, y, 1 - c))


def ring(value):
    return along_band(value, lambda x, y, c: (x, y + 1 - 2 * c, c))


def against_ring(value):
    return along_band(value, lambda x, y, c: (x, y - 1 + 2 * c, c))


def to_other_x(value):
    return along_band(value, lambda x, y, c: (x + 1, y, c))


def near_exchange(value):
    groups = [[zh * NEAR + n for n in range(NEAR)] for zh in range(N_Z_HI)]
    return lax.all_to_all(value, "coef", 0, 0, axis_index_groups=groups, tiled=True)


def far_exchange(value):
    groups = [
        [(zh * NEAR + n) * N_BAND + chip * 2 + core for zh in range(N_Z_HI) for core in range(2)]
        for n in range(NEAR) for chip in range(N_BAND // 2)
    ]
    return lax.all_to_all(value, ("coef", "band"), 0, 0, axis_index_groups=groups, tiled=True)


def on_device(wave, projector, gvec, atom_of, dion, qaug):
    b, c = lax.axis_index("band"), lax.axis_index("coef")
    x, y, core, z_hi = b >> 3, (b >> 1) & 3, b & 1, c >> 3
    order = [y, (y + 3 + 2 * core) & 3, (y + 1 + 2 * core) & 3, (y + 2) & 3]
    place = jnp.stack(
        [core, z_hi] + [x * 4 + at for at in order] + [(1 - x) * 4 + at for at in order]).astype(jnp.int32)

    across = to_other_x(projector)
    before, after = ring(projector), against_ring(projector)
    far = ring(before)
    stat, wave_v = stats(wave, gvec)
    across, after, far, own_wave, stat, late_dion = lax.optimization_barrier((across, after, far, wave, stat, dion))
    far_x = to_other_x(far)
    before_x, after_x = ring(across), against_ring(across)
    wave_other = swap(own_wave)
    shards = [projector, before, after, far, across, before_x, after_x, far_x]
    weights = masked_weights(atom_of, late_dion, qaug)
    stat, weights = lax.optimization_barrier((stat, weights))
    message, whole = intersect(place, stat, wave_v, wave_other, shards)

    keep, message = near_sum(place, near_exchange(message))
    coupled = near_exchange(couple(place, keep, far_exchange(message), weights))
    return finish(place, coupled, wave_v, gvec, whole, swap(whole))


def solution(mesh):
    in_specs = (P("band", "coef"), P("band", "coef"), P(None, "coef"), P(), P(), P())
    out_specs = P("band", "coef")
    return jax.shard_map(
        on_device, mesh=mesh, in_specs=in_specs, out_specs=out_specs, check_vma=False
    )
```

```python
import functools
import jax
import jax.numpy as jnp
from jax import lax
from jax.experimental import pallas as pl
from jax.experimental.pallas import tpu as pltpu
from jax.sharding import PartitionSpec as P

kinetic_unit = 0.005
f32 = jnp.float32
bf16 = jnp.bfloat16

N_COEF = 32
N_BAND = 16
ROWS = 256
COLS = 4096
NPROJ = 512
SHARD = NPROJ // N_BAND
HALF_PROJ = NPROJ // 2
QUARTER_PROJ = NPROJ // 4
NEAR = 8
BANDS = ROWS // NEAR
STAT_ROWS = BANDS // 4
NEAR_ROWS = 2 * BANDS + STAT_ROWS
FAR_ROWS = BANDS + STAT_ROWS
N_Z_HI = N_COEF // NEAR
FAR = 2 * N_Z_HI

anywhere = pl.BlockSpec(memory_space=pl.ANY)
vmem = pl.BlockSpec(memory_space=pltpu.VMEM)
smem = pl.BlockSpec(memory_space=pltpu.SMEM)

CORE, Z_HI, ORDER = 0, 1, 2


def in_vmem(value):
    return pltpu.with_memory_space_constraint(value, pltpu.VMEM)


def in_hbm(value):
    return pltpu.with_memory_space_constraint(value, pltpu.HBM)


def params(mib):
    return pltpu.CompilerParams(vmem_limit_bytes=mib * 1024 * 1024)


def cost(flops, bytes_accessed):
    return pl.CostEstimate(flops=flops, bytes_accessed=bytes_accessed, transcendentals=0)


def pieces(value):
    hi = value.astype(bf16).astype(f32)
    rest = value - hi
    mid = rest.astype(bf16).astype(f32)
    lo = (rest - mid).astype(bf16).astype(f32)
    return hi, mid, lo


def stat_lanes():
    return lax.broadcasted_iota(jnp.int32, (STAT_ROWS, HALF_PROJ), 1)


def split_rows(value):
    lane = stat_lanes() & 63
    hi, mid, lo = [jnp.where((lane == 0) | (lane == 3), piece, 0.0) for piece in pieces(value)]
    return hi + pltpu.roll(mid, 1, 1) + pltpu.roll(lo, 2, 1)


def join_rows(packed):
    return packed + pltpu.roll(packed, HALF_PROJ - 1, 1) + pltpu.roll(packed, HALF_PROJ - 2, 1)


def to_rows(first, second):
    lane = stat_lanes()
    out = jnp.zeros((STAT_ROWS, HALF_PROJ), f32)
    for k in range(4):
        rows = slice(k * STAT_ROWS, (k + 1) * STAT_ROWS)
        out = jnp.where(lane == 64 * k, first[rows], jnp.where(lane == 64 * k + 3, second[rows], out))
    return split_rows(out)


def from_rows(packed):
    lane = stat_lanes()
    columns = []
    for begin in (0, 3):
        columns.append(jnp.concatenate([
            jnp.sum(jnp.where((lane >= 64 * k + begin) & (lane < 64 * k + begin + 3), packed, 0.0), axis=1, keepdims=True)
            for k in range(4)
        ], axis=0))
    return columns


def kinetic(gvec):
    comps = gvec.astype(f32)
    return kinetic_unit * (comps[0:1] * comps[0:1] + comps[1:2] * comps[1:2] + comps[2:3] * comps[2:3])


def stats_kernel(wave, gvec, stat, wave_v, sems):
    copies = [
        pltpu.make_async_copy(
            wave.at[pl.ds(n * BANDS, BANDS), :], wave_v.at[pl.ds(n * BANDS, BANDS), :], sems.at[n])
        for n in range(NEAR)
    ]
    for copy in copies:
        copy.start()
    kin = kinetic(gvec[...])
    for n, copy in enumerate(copies):
        copy.wait()
        value = wave_v[n * BANDS:(n + 1) * BANDS, :].astype(f32)
        square = value * value
        sq = jnp.sum(square, axis=1, keepdims=True)
        ksq = jnp.sum(square * kin, axis=1, keepdims=True)
        stat[n * STAT_ROWS:(n + 1) * STAT_ROWS, :] = to_rows(sq, ksq)


def stats(wave, gvec):
    return pl.pallas_call(
        stats_kernel,
        in_specs=[anywhere, vmem],
        out_specs=[vmem, vmem],
        out_shape=[
            jax.ShapeDtypeStruct((NEAR * STAT_ROWS, HALF_PROJ), f32),
            pltpu.VMEM((ROWS, COLS), bf16),
        ],
        scratch_shapes=[pltpu.SemaphoreType.DMA((NEAR,))],
        compiler_params=params(16),
        cost_estimate=cost(5 * ROWS * COLS, 2 * ROWS * COLS),
        name="stats",
    )(in_hbm(wave), gvec)


def weights_kernel(atom_of, dion, qaug, out):
    number = lax.broadcasted_iota(jnp.int32, (64, NPROJ), 0)
    member = jnp.where(atom_of[...] == number, 1.0, 0.0).astype(bf16)
    same = lax.dot_general(member, member, (((0,), (0,)), ((), ())), preferred_element_type=f32) > 0.5
    to = lax.broadcasted_iota(jnp.int32, (NPROJ, NPROJ), 0)
    source = ((to & 0xE0) << 1) | ((to >> 8) << 5) | (to & 31)
    order = jnp.where(source == lax.broadcasted_iota(jnp.int32, (NPROJ, NPROJ), 1), 1.0, 0.0).astype(bf16)
    for at, matrix in enumerate((dion, qaug)):
        value = jnp.where(same, matrix[...].astype(f32), 0.0).astype(bf16)
        rows = jnp.dot(order, value, preferred_element_type=f32).astype(bf16)
        out[:, at * NPROJ:(at + 1) * NPROJ] = lax.dot_general(
            rows, order, (((1,), (1,)), ((), ())), preferred_element_type=f32).astype(bf16)


def masked_weights(atom_of, dion, qaug):
    return pl.pallas_call(
        weights_kernel,
        in_specs=[vmem] * 3,
        out_specs=vmem,
        out_shape=jax.ShapeDtypeStruct((NPROJ, 2 * NPROJ), bf16),
        compiler_params=params(24),
        cost_estimate=cost(9 * NPROJ ** 3, 8 * NPROJ * NPROJ),
        name="masked_weights",
    )(atom_of.reshape(1, NPROJ), in_hbm(dion), in_hbm(qaug))


def against(left, right):
    return lax.dot_general(left, right, (((1,), (1,)), ((), ())), preferred_element_type=f32)


N_SHARDS = HALF_PROJ // SHARD


def intersect_kernel(place, stat, wave_own, wave_other, *refs):
    shards = refs[:N_SHARDS]
    message, whole, whole_v, message_v, out_sem = refs[N_SHARDS:]
    for i, shard in enumerate(shards):
        at = pl.multiple_of(place[ORDER + i] * SHARD, SHARD)
        whole_v[pl.ds(at, SHARD), :] = shard[...]
    back = pltpu.make_async_copy(whole_v, whole, out_sem)
    back.start()
    for core, wave in enumerate((wave_own, wave_other)):
        total = against(wave[...], whole_v[...])
        for n in range(NEAR):
            at = n * NEAR_ROWS + core * BANDS
            message_v[at:at + BANDS, :] = total[n * BANDS:(n + 1) * BANDS]
    for n in range(NEAR):
        at = n * NEAR_ROWS + 2 * BANDS
        message_v[at:at + STAT_ROWS, :] = stat[n * STAT_ROWS:(n + 1) * STAT_ROWS, :]
    message[...] = message_v[...].astype(bf16)
    back.wait()


def intersect(place, stat, wave_own, wave_other, shards):
    return pl.pallas_call(
        intersect_kernel,
        in_specs=[smem] + [vmem] * (3 + N_SHARDS),
        out_specs=[vmem, anywhere],
        out_shape=[
            jax.ShapeDtypeStruct((NEAR * NEAR_ROWS, HALF_PROJ), bf16),
            pltpu.HBM((HALF_PROJ, COLS), bf16),
        ],
        scratch_shapes=[
            pltpu.VMEM((HALF_PROJ, COLS), bf16),
            pltpu.VMEM((NEAR * NEAR_ROWS, HALF_PROJ), f32),
            pltpu.SemaphoreType.DMA,
        ],
        compiler_params=params(24),
        cost_estimate=cost(4 * ROWS * COLS * HALF_PROJ, 2 * (2 * ROWS + 2 * HALF_PROJ) * COLS),
        name="intersect",
    )(place, stat, in_vmem(wave_own), in_vmem(wave_other), *[in_vmem(shard) for shard in shards])


def near_sum_kernel(place, received, keep, message, message_v):
    total = jnp.sum(received[...].astype(f32).reshape(NEAR, NEAR_ROWS, HALF_PROJ), axis=0)
    keep[...] = total[:BANDS]
    rows = split_rows(join_rows(total[2 * BANDS:]))
    core = place[CORE]
    for zh in range(N_Z_HI):
        for c, value in ((core, total[:BANDS]), (1 - core, total[BANDS:2 * BANDS])):
            at = pl.multiple_of((zh * 2 + c) * FAR_ROWS, STAT_ROWS)
            message_v[pl.ds(at, BANDS), :] = value
            message_v[pl.ds(at + BANDS, STAT_ROWS), :] = rows
    message[...] = message_v[...].astype(bf16)


def near_sum(place, received):
    return pl.pallas_call(
        near_sum_kernel,
        in_specs=[smem, vmem],
        out_specs=[vmem, vmem],
        out_shape=[
            jax.ShapeDtypeStruct((BANDS, HALF_PROJ), f32),
            jax.ShapeDtypeStruct((FAR * FAR_ROWS, HALF_PROJ), bf16),
        ],
        scratch_shapes=[pltpu.VMEM((FAR * FAR_ROWS, HALF_PROJ), f32)],
        compiler_params=params(16),
        cost_estimate=cost(NEAR * NEAR_ROWS * HALF_PROJ, 3 * NEAR * NEAR_ROWS * HALF_PROJ),
        name="near_sum",
    )(place, received)


def couple_kernel(place, keep, received, weights, out):
    blocks = received[...].astype(f32).reshape(FAR, FAR_ROWS, HALF_PROJ)
    core = place[CORE]
    own_at = place[Z_HI] * 2 + core
    halves, packed = [], []
    for c in range(2):
        total = jnp.zeros((BANDS, HALF_PROJ), f32)
        rows = jnp.zeros((STAT_ROWS, HALF_PROJ), f32)
        for zh in range(N_Z_HI):
            block = blocks[zh * 2 + c]
            total += jnp.where(own_at == zh * 2 + c, keep[...], block[:BANDS])
            rows += block[BANDS:]
        halves.append(total)
        packed.append(rows)
    inter = jnp.concatenate(halves, axis=1)
    sq, ksq = from_rows(jnp.where(core == 0, packed[0], packed[1]))
    stacked = jnp.concatenate(pieces(inter), axis=0).astype(bf16)
    both = jnp.dot(stacked, weights[...], preferred_element_type=f32)
    both = both[:BANDS] + (both[BANDS:2 * BANDS] + both[2 * BANDS:])
    pd, pq = both[:, :NPROJ], both[:, NPROJ:]
    energy = (ksq + jnp.sum(inter * pd, axis=1, keepdims=True)) / (
        sq + jnp.sum(inter * pq, axis=1, keepdims=True))
    ekin = ksq / (sq + 1e-6)
    coupled = pd - energy * pq
    block = jnp.concatenate([coupled[:, :HALF_PROJ], coupled[:, HALF_PROJ:], to_rows(energy, ekin)], axis=0)
    out[...] = jnp.concatenate([block] * NEAR, axis=0).astype(bf16)


def couple(place, keep, received, weights):
    return pl.pallas_call(
        couple_kernel,
        in_specs=[smem] + [vmem] * 3,
        out_specs=vmem,
        out_shape=jax.ShapeDtypeStruct((NEAR * NEAR_ROWS, HALF_PROJ), bf16),
        compiler_params=params(16),
        cost_estimate=cost(12 * BANDS * NPROJ * NPROJ, 4 * NPROJ * NPROJ + 4 * ROWS * NPROJ),
        name="couple",
    )(place, keep, received, weights)


TILE = 512
N_TILES = COLS // TILE
CHUNK = 16


def finish_kernel(place, coupled, gvec, wave, whole_own, whole_other, out,
                  whole_v, out_v, halves_v, energy_v, scale_v, even_v, odd_v, sems, out_sems):
    def columns(tile):
        return slice(tile * TILE, (tile + 1) * TILE)

    def copies(tile):
        cols = columns(tile)
        return [
            pltpu.make_async_copy(
                source.at[:, cols], whole_v.at[pl.ds(i * HALF_PROJ, HALF_PROJ), cols], sems.at[tile, i])
            for i, source in enumerate((whole_own, whole_other))
        ]

    def out_copy(tile):
        cols = columns(tile)
        return pltpu.make_async_copy(out_v.at[:, cols], out.at[:, cols], out_sems.at[tile])

    def arrive(tile):
        for copy in copies(tile):
            copy.wait()

    def expand(tile, expanded_v):
        cols = columns(tile)
        expanded_v[...] = jnp.dot(halves_v[...], whole_v[:, cols], preferred_element_type=f32)

    def conclude(tile, expanded_v):
        cols = columns(tile)
        kin = jnp.broadcast_to(kinetic(gvec[:, cols]), (CHUNK, TILE))
        for i in range(ROWS // CHUNK):
            rows = slice(i * CHUNK, (i + 1) * CHUNK)
            energy = jnp.concatenate([energy_v[rows, :]] * (TILE // 128), axis=1)
            scale = jnp.concatenate([scale_v[rows, :]] * (TILE // 128), axis=1)
            resid = (kin - energy) * wave[rows, cols].astype(f32) + expanded_v[rows, :]
            t = kin * scale
            square = t * t
            num = (3.0 + t) * (9.0 + square)
            inverse = pl.reciprocal(num + square * square, approx=True)
            out_v[rows, cols] = ((num * inverse) * resid).astype(bf16)

    def depart(tiles):
        for tile in tiles:
            for copy in copies(tile):
                copy.start()

    depart(range(3))
    core = place[CORE]
    blocks = coupled[...].astype(f32).reshape(NEAR, NEAR_ROWS, HALF_PROJ)
    for n in range(NEAR):
        rows = slice(n * BANDS, (n + 1) * BANDS)
        first, second = blocks[n, :BANDS].astype(bf16), blocks[n, BANDS:2 * BANDS].astype(bf16)
        halves_v[rows, :HALF_PROJ] = jnp.where(core == 0, first, second)
        halves_v[rows, HALF_PROJ:] = jnp.where(core == 0, second, first)
        energy, ekin = from_rows(blocks[n, 2 * BANDS:])
        energy_v[rows, :] = jnp.broadcast_to(energy, (BANDS, 128))
        scale_v[rows, :] = jnp.broadcast_to(2.0 / ekin, (BANDS, 128))
    depart(range(3, N_TILES))
    arrive(0)
    expand(0, even_v)

    buffers = (even_v, odd_v)
    for tile in range(N_TILES):
        if tile + 1 < N_TILES:
            arrive(tile + 1)
            expand(tile + 1, buffers[(tile + 1) % 2])
        conclude(tile, buffers[tile % 2])
        out_copy(tile).start()

    for tile in range(N_TILES):
        out_copy(tile).wait()


def finish(place, coupled, wave, gvec, whole_own, whole_other):
    return pl.pallas_call(
        finish_kernel,
        in_specs=[smem] + [vmem] * 3 + [anywhere] * 2,
        out_specs=anywhere,
        out_shape=jax.ShapeDtypeStruct((ROWS, COLS), bf16),
        scratch_shapes=[pltpu.VMEM((NPROJ, COLS), bf16), pltpu.VMEM((ROWS, COLS), bf16), pltpu.VMEM((ROWS, NPROJ), bf16)]
        + [pltpu.VMEM((ROWS, 128), f32)] * 2 + [pltpu.VMEM((ROWS, TILE), f32)] * 2
        + [pltpu.SemaphoreType.DMA((N_TILES, 2)), pltpu.SemaphoreType.DMA((N_TILES,))],
        compiler_params=params(24),
        cost_estimate=cost(2 * ROWS * COLS * NPROJ, 2 * (2 * ROWS + NPROJ) * COLS),
        name="finish",
    )(place, coupled, gvec, in_vmem(wave), in_hbm(whole_own), whole_other)


def band_perm(move):
    pairs = []
    for b in range(N_BAND):
        x, y, c = move(b // 8, (b // 2) % 4, b % 2)
        pairs.append((b, (x % 2) * 8 + (y % 4) * 2 + c))
    return pairs


def along_band(value, move):
    return lax.ppermute(value, "band", band_perm(move))


def swap(value):
    return along_band(value, lambda x, y, c: (x, y, 1 - c))


def ring(value):
    return along_band(value, lambda x, y, c: (x, y + 1 - 2 * c, c))


def against_ring(value):
    return along_band(value, lambda x, y, c: (x, y - 1 + 2 * c, c))


def to_other_x(value):
    return along_band(value, lambda x, y, c: (x + 1, y, c))


def near_exchange(value):
    groups = [[zh * NEAR + n for n in range(NEAR)] for zh in range(N_Z_HI)]
    return lax.all_to_all(value, "coef", 0, 0, axis_index_groups=groups, tiled=True)


def far_exchange(value):
    groups = [
        [(zh * NEAR + n) * N_BAND + chip * 2 + core for zh in range(N_Z_HI) for core in range(2)]
        for n in range(NEAR) for chip in range(N_BAND // 2)
    ]
    return lax.all_to_all(value, ("coef", "band"), 0, 0, axis_index_groups=groups, tiled=True)


def on_device(wave, projector, gvec, atom_of, dion, qaug):
    b, c = lax.axis_index("band"), lax.axis_index("coef")
    x, y, core, z_hi = b >> 3, (b >> 1) & 3, b & 1, c >> 3
    order = [y, (y + 3 + 2 * core) & 3, (y + 1 + 2 * core) & 3, (y + 2) & 3]
    place = jnp.stack(
        [core, z_hi] + [x * 4 + at for at in order] + [(1 - x) * 4 + at for at in order]).astype(jnp.int32)

    across = to_other_x(projector)
    before, after = ring(projector), against_ring(projector)
    far = ring(before)
    stat, wave_v = stats(wave, gvec)
    across, after, far, own_wave, stat, late_dion = lax.optimization_barrier((across, after, far, wave, stat, dion))
    far_x = to_other_x(far)
    before_x, after_x = ring(across), against_ring(across)
    wave_other = swap(own_wave)
    shards = [projector, before, after, far, across, before_x, after_x, far_x]
    weights = masked_weights(atom_of, late_dion, qaug)
    stat, weights = lax.optimization_barrier((stat, weights))
    message, whole = intersect(place, stat, wave_v, wave_other, shards)

    keep, message = near_sum(place, near_exchange(message))
    coupled = near_exchange(couple(place, keep, far_exchange(message), weights))
    return finish(place, coupled, wave_v, gvec, whole, swap(whole))


def solution(mesh):
    in_specs = (P("band", "coef"), P("band", "coef"), P(None, "coef"), P(), P(), P())
    out_specs = P("band", "coef")
    return jax.shard_map(
        on_device, mesh=mesh, in_specs=in_specs, out_specs=out_specs, check_vma=False
    )
```

```python
import functools
import jax
import jax.numpy as jnp
from jax import lax
from jax.experimental import pallas as pl
from jax.experimental.pallas import tpu as pltpu
from jax.sharding import PartitionSpec as P

kinetic_unit = 0.005
f32 = jnp.float32
bf16 = jnp.bfloat16

N_COEF = 32
N_BAND = 16
ROWS = 256
COLS = 4096
NPROJ = 512
SHARD = NPROJ // N_BAND
HALF_PROJ = NPROJ // 2
QUARTER_PROJ = NPROJ // 4
NEAR = 8
BANDS = ROWS // NEAR
STAT_ROWS = BANDS // 4
NEAR_ROWS = 2 * BANDS + STAT_ROWS
FAR_ROWS = BANDS + STAT_ROWS
N_Z_HI = N_COEF // NEAR
FAR = 2 * N_Z_HI

anywhere = pl.BlockSpec(memory_space=pl.ANY)
vmem = pl.BlockSpec(memory_space=pltpu.VMEM)
smem = pl.BlockSpec(memory_space=pltpu.SMEM)

CORE, Z_HI, ORDER = 0, 1, 2


def in_vmem(value):
    return pltpu.with_memory_space_constraint(value, pltpu.VMEM)


def in_hbm(value):
    return pltpu.with_memory_space_constraint(value, pltpu.HBM)


def params(mib):
    return pltpu.CompilerParams(vmem_limit_bytes=mib * 1024 * 1024)


def cost(flops, bytes_accessed):
    return pl.CostEstimate(flops=flops, bytes_accessed=bytes_accessed, transcendentals=0)


def pieces(value):
    hi = value.astype(bf16).astype(f32)
    rest = value - hi
    mid = rest.astype(bf16).astype(f32)
    lo = (rest - mid).astype(bf16).astype(f32)
    return hi, mid, lo


def stat_lanes():
    return lax.broadcasted_iota(jnp.int32, (STAT_ROWS, HALF_PROJ), 1)


def split_rows(value):
    lane = stat_lanes() & 63
    hi, mid, lo = [jnp.where((lane == 0) | (lane == 3), piece, 0.0) for piece in pieces(value)]
    return hi + pltpu.roll(mid, 1, 1) + pltpu.roll(lo, 2, 1)


def join_rows(packed):
    return packed + pltpu.roll(packed, HALF_PROJ - 1, 1) + pltpu.roll(packed, HALF_PROJ - 2, 1)


def to_rows(first, second):
    lane = stat_lanes()
    out = jnp.zeros((STAT_ROWS, HALF_PROJ), f32)
    for k in range(4):
        rows = slice(k * STAT_ROWS, (k + 1) * STAT_ROWS)
        out = jnp.where(lane == 64 * k, first[rows], jnp.where(lane == 64 * k + 3, second[rows], out))
    return split_rows(out)


def from_rows(packed):
    lane = stat_lanes()
    columns = []
    for begin in (0, 3):
        columns.append(jnp.concatenate([
            jnp.sum(jnp.where((lane >= 64 * k + begin) & (lane < 64 * k + begin + 3), packed, 0.0), axis=1, keepdims=True)
            for k in range(4)
        ], axis=0))
    return columns


def kinetic(gvec):
    comps = gvec.astype(f32)
    return kinetic_unit * (comps[0:1] * comps[0:1] + comps[1:2] * comps[1:2] + comps[2:3] * comps[2:3])


def stats_kernel(wave, gvec, stat, wave_v, sems):
    copies = [
        pltpu.make_async_copy(
            wave.at[pl.ds(n * BANDS, BANDS), :], wave_v.at[pl.ds(n * BANDS, BANDS), :], sems.at[n])
        for n in range(NEAR)
    ]
    for copy in copies:
        copy.start()
    kin = kinetic(gvec[...])
    for n, copy in enumerate(copies):
        copy.wait()
        value = wave_v[n * BANDS:(n + 1) * BANDS, :].astype(f32)
        square = value * value
        sq = jnp.sum(square, axis=1, keepdims=True)
        ksq = jnp.sum(square * kin, axis=1, keepdims=True)
        stat[n * STAT_ROWS:(n + 1) * STAT_ROWS, :] = to_rows(sq, ksq)


def stats(wave, gvec):
    return pl.pallas_call(
        stats_kernel,
        in_specs=[anywhere, vmem],
        out_specs=[vmem, vmem],
        out_shape=[
            jax.ShapeDtypeStruct((NEAR * STAT_ROWS, HALF_PROJ), f32),
            pltpu.VMEM((ROWS, COLS), bf16),
        ],
        scratch_shapes=[pltpu.SemaphoreType.DMA((NEAR,))],
        compiler_params=params(16),
        cost_estimate=cost(5 * ROWS * COLS, 2 * ROWS * COLS),
        name="stats",
    )(in_hbm(wave), gvec)


def weights_kernel(atom_of, dion, qaug, out):
    number = lax.broadcasted_iota(jnp.int32, (64, NPROJ), 0)
    member = jnp.where(atom_of[...] == number, 1.0, 0.0).astype(bf16)
    same = lax.dot_general(member, member, (((0,), (0,)), ((), ())), preferred_element_type=f32) > 0.5
    to = lax.broadcasted_iota(jnp.int32, (NPROJ, NPROJ), 0)
    source = ((to & 0xE0) << 1) | ((to >> 8) << 5) | (to & 31)
    order = jnp.where(source == lax.broadcasted_iota(jnp.int32, (NPROJ, NPROJ), 1), 1.0, 0.0).astype(bf16)
    for at, matrix in enumerate((dion, qaug)):
        value = jnp.where(same, matrix[...].astype(f32), 0.0).astype(bf16)
        rows = jnp.dot(order, value, preferred_element_type=f32).astype(bf16)
        out[:, at * NPROJ:(at + 1) * NPROJ] = lax.dot_general(
            rows, order, (((1,), (1,)), ((), ())), preferred_element_type=f32).astype(bf16)


def masked_weights(atom_of, dion, qaug):
    return pl.pallas_call(
        weights_kernel,
        in_specs=[vmem] * 3,
        out_specs=vmem,
        out_shape=jax.ShapeDtypeStruct((NPROJ, 2 * NPROJ), bf16),
        compiler_params=params(24),
        cost_estimate=cost(9 * NPROJ ** 3, 8 * NPROJ * NPROJ),
        name="masked_weights",
    )(atom_of.reshape(1, NPROJ), in_hbm(dion), in_hbm(qaug))


def against(left, right):
    return lax.dot_general(left, right, (((1,), (1,)), ((), ())), preferred_element_type=f32)


N_SHARDS = HALF_PROJ // SHARD


def intersect_kernel(place, stat, wave_own, wave_other, *refs):
    shards = refs[:N_SHARDS]
    message, whole, whole_v, message_v, out_sem = refs[N_SHARDS:]
    for i, shard in enumerate(shards):
        at = pl.multiple_of(place[ORDER + i] * SHARD, SHARD)
        whole_v[pl.ds(at, SHARD), :] = shard[...]
    back = pltpu.make_async_copy(whole_v, whole, out_sem)
    back.start()
    for core, wave in enumerate((wave_own, wave_other)):
        total = against(wave[...], whole_v[...])
        for n in range(NEAR):
            at = n * NEAR_ROWS + core * BANDS
            message_v[at:at + BANDS, :] = total[n * BANDS:(n + 1) * BANDS]
    for n in range(NEAR):
        at = n * NEAR_ROWS + 2 * BANDS
        message_v[at:at + STAT_ROWS, :] = stat[n * STAT_ROWS:(n + 1) * STAT_ROWS, :]
    message[...] = message_v[...].astype(bf16)
    back.wait()


def intersect(place, stat, wave_own, wave_other, shards):
    return pl.pallas_call(
        intersect_kernel,
        in_specs=[smem] + [vmem] * (3 + N_SHARDS),
        out_specs=[vmem, anywhere],
        out_shape=[
            jax.ShapeDtypeStruct((NEAR * NEAR_ROWS, HALF_PROJ), bf16),
            pltpu.HBM((HALF_PROJ, COLS), bf16),
        ],
        scratch_shapes=[
            pltpu.VMEM((HALF_PROJ, COLS), bf16),
            pltpu.VMEM((NEAR * NEAR_ROWS, HALF_PROJ), f32),
            pltpu.SemaphoreType.DMA,
        ],
        compiler_params=params(24),
        cost_estimate=cost(4 * ROWS * COLS * HALF_PROJ, 2 * (2 * ROWS + 2 * HALF_PROJ) * COLS),
        name="intersect",
    )(place, stat, in_vmem(wave_own), in_vmem(wave_other), *[in_vmem(shard) for shard in shards])


def near_sum_kernel(place, received, keep, message, message_v):
    total = jnp.sum(received[...].astype(f32).reshape(NEAR, NEAR_ROWS, HALF_PROJ), axis=0)
    keep[...] = total[:BANDS]
    rows = split_rows(join_rows(total[2 * BANDS:]))
    core = place[CORE]
    for zh in range(N_Z_HI):
        for c, value in ((core, total[:BANDS]), (1 - core, total[BANDS:2 * BANDS])):
            at = pl.multiple_of((zh * 2 + c) * FAR_ROWS, STAT_ROWS)
            message_v[pl.ds(at, BANDS), :] = value
            message_v[pl.ds(at + BANDS, STAT_ROWS), :] = rows
    message[...] = message_v[...].astype(bf16)


def near_sum(place, received):
    return pl.pallas_call(
        near_sum_kernel,
        in_specs=[smem, vmem],
        out_specs=[vmem, vmem],
        out_shape=[
            jax.ShapeDtypeStruct((BANDS, HALF_PROJ), f32),
            jax.ShapeDtypeStruct((FAR * FAR_ROWS, HALF_PROJ), bf16),
        ],
        scratch_shapes=[pltpu.VMEM((FAR * FAR_ROWS, HALF_PROJ), f32)],
        compiler_params=params(16),
        cost_estimate=cost(NEAR * NEAR_ROWS * HALF_PROJ, 3 * NEAR * NEAR_ROWS * HALF_PROJ),
        name="near_sum",
    )(place, received)


def couple_kernel(place, keep, received, weights, out):
    blocks = received[...].astype(f32).reshape(FAR, FAR_ROWS, HALF_PROJ)
    core = place[CORE]
    own_at = place[Z_HI] * 2 + core
    halves, packed = [], []
    for c in range(2):
        total = jnp.zeros((BANDS, HALF_PROJ), f32)
        rows = jnp.zeros((STAT_ROWS, HALF_PROJ), f32)
        for zh in range(N_Z_HI):
            block = blocks[zh * 2 + c]
            total += jnp.where(own_at == zh * 2 + c, keep[...], block[:BANDS])
            rows += block[BANDS:]
        halves.append(total)
        packed.append(rows)
    inter = jnp.concatenate(halves, axis=1)
    sq, ksq = from_rows(jnp.where(core == 0, packed[0], packed[1]))
    stacked = jnp.concatenate(pieces(inter), axis=0).astype(bf16)
    both = jnp.dot(stacked, weights[...], preferred_element_type=f32)
    both = both[:BANDS] + (both[BANDS:2 * BANDS] + both[2 * BANDS:])
    pd, pq = both[:, :NPROJ], both[:, NPROJ:]
    energy = (ksq + jnp.sum(inter * pd, axis=1, keepdims=True)) / (
        sq + jnp.sum(inter * pq, axis=1, keepdims=True))
    ekin = ksq / (sq + 1e-6)
    coupled = pd - energy * pq
    block = jnp.concatenate([coupled[:, :HALF_PROJ], coupled[:, HALF_PROJ:], to_rows(energy, ekin)], axis=0)
    out[...] = jnp.concatenate([block] * NEAR, axis=0).astype(bf16)


def couple(place, keep, received, weights):
    return pl.pallas_call(
        couple_kernel,
        in_specs=[smem] + [vmem] * 3,
        out_specs=vmem,
        out_shape=jax.ShapeDtypeStruct((NEAR * NEAR_ROWS, HALF_PROJ), bf16),
        compiler_params=params(16),
        cost_estimate=cost(12 * BANDS * NPROJ * NPROJ, 4 * NPROJ * NPROJ + 4 * ROWS * NPROJ),
        name="couple",
    )(place, keep, received, weights)


TILE = 512
N_TILES = COLS // TILE
CHUNK = 16


def finish_kernel(place, coupled, gvec, wave, whole_own, whole_other, out,
                  whole_v, out_v, halves_v, energy_v, scale_v, even_v, odd_v, sems, out_sems):
    def columns(tile):
        return pl.ds(pl.multiple_of(tile * TILE, TILE), TILE)

    def copies(tile):
        cols = columns(tile)
        return [
            pltpu.make_async_copy(
                source.at[:, cols], whole_v.at[pl.ds(i * HALF_PROJ, HALF_PROJ), cols], sems.at[tile, i])
            for i, source in enumerate((whole_own, whole_other))
        ]

    def out_copy(tile):
        cols = columns(tile)
        return pltpu.make_async_copy(out_v.at[:, cols], out.at[:, cols], out_sems.at[tile])

    def arrive(tile):
        for copy in copies(tile):
            copy.wait()

    def expand(tile, expanded_v):
        cols = columns(tile)
        expanded_v[...] = jnp.dot(halves_v[...], whole_v[:, cols], preferred_element_type=f32)

    def conclude(tile, expanded_v):
        cols = columns(tile)
        kin = jnp.broadcast_to(kinetic(gvec[:, cols]), (CHUNK, TILE))
        for i in range(ROWS // CHUNK):
            rows = slice(i * CHUNK, (i + 1) * CHUNK)
            energy = jnp.concatenate([energy_v[rows, :]] * (TILE // 128), axis=1)
            scale = jnp.concatenate([scale_v[rows, :]] * (TILE // 128), axis=1)
            resid = (kin - energy) * wave[rows, cols].astype(f32) + expanded_v[rows, :]
            t = kin * scale
            square = t * t
            num = (3.0 + t) * (9.0 + square)
            inverse = pl.reciprocal(num + square * square, approx=True)
            out_v[rows, cols] = ((num * inverse) * resid).astype(bf16)

    def depart(tiles):
        for tile in tiles:
            for copy in copies(tile):
                copy.start()

    depart(range(3))
    core = place[CORE]
    blocks = coupled[...].astype(f32).reshape(NEAR, NEAR_ROWS, HALF_PROJ)
    for n in range(NEAR):
        rows = slice(n * BANDS, (n + 1) * BANDS)
        first, second = blocks[n, :BANDS].astype(bf16), blocks[n, BANDS:2 * BANDS].astype(bf16)
        halves_v[rows, :HALF_PROJ] = jnp.where(core == 0, first, second)
        halves_v[rows, HALF_PROJ:] = jnp.where(core == 0, second, first)
        energy, ekin = from_rows(blocks[n, 2 * BANDS:])
        energy_v[rows, :] = jnp.broadcast_to(energy, (BANDS, 128))
        scale_v[rows, :] = jnp.broadcast_to(2.0 / ekin, (BANDS, 128))
    depart(range(3, N_TILES))
    arrive(0)
    expand(0, even_v)

    @pl.loop(0, N_TILES // 2)
    def _(i):
        arrive(2 * i + 1)

        @pl.when(i + 1 < N_TILES // 2)
        def _():
            arrive(2 * i + 2)

        expand(2 * i + 1, odd_v)
        conclude(2 * i, even_v)
        out_copy(2 * i).start()
        expand(jnp.minimum(2 * i + 2, N_TILES - 1), even_v)
        conclude(2 * i + 1, odd_v)
        out_copy(2 * i + 1).start()

    for tile in range(N_TILES):
        out_copy(tile).wait()


def finish(place, coupled, wave, gvec, whole_own, whole_other):
    return pl.pallas_call(
        finish_kernel,
        in_specs=[smem] + [vmem] * 3 + [anywhere] * 2,
        out_specs=anywhere,
        out_shape=jax.ShapeDtypeStruct((ROWS, COLS), bf16),
        scratch_shapes=[pltpu.VMEM((NPROJ, COLS), bf16), pltpu.VMEM((ROWS, COLS), bf16), pltpu.VMEM((ROWS, NPROJ), bf16)]
        + [pltpu.VMEM((ROWS, 128), f32)] * 2 + [pltpu.VMEM((ROWS, TILE), f32)] * 2
        + [pltpu.SemaphoreType.DMA((N_TILES, 2)), pltpu.SemaphoreType.DMA((N_TILES,))],
        compiler_params=params(24),
        cost_estimate=cost(2 * ROWS * COLS * NPROJ, 2 * (2 * ROWS + NPROJ) * COLS),
        name="finish",
    )(place, coupled, gvec, in_vmem(wave), in_hbm(whole_own), whole_other)


def band_perm(move):
    pairs = []
    for b in range(N_BAND):
        x, y, c = move(b // 8, (b // 2) % 4, b % 2)
        pairs.append((b, (x % 2) * 8 + (y % 4) * 2 + c))
    return pairs


def along_band(value, move):
    return lax.ppermute(value, "band", band_perm(move))


def swap(value):
    return along_band(value, lambda x, y, c: (x, y, 1 - c))


def ring(value):
    return along_band(value, lambda x, y, c: (x, y + 1 - 2 * c, c))


def against_ring(value):
    return along_band(value, lambda x, y, c: (x, y - 1 + 2 * c, c))


def to_other_x(value):
    return along_band(value, lambda x, y, c: (x + 1, y, c))


def near_exchange(value):
    groups = [[zh * NEAR + n for n in range(NEAR)] for zh in range(N_Z_HI)]
    return lax.all_to_all(value, "coef", 0, 0, axis_index_groups=groups, tiled=True)


def far_exchange(value):
    groups = [
        [(zh * NEAR + n) * N_BAND + chip * 2 + core for zh in range(N_Z_HI) for core in range(2)]
        for n in range(NEAR) for chip in range(N_BAND // 2)
    ]
    return lax.all_to_all(value, ("coef", "band"), 0, 0, axis_index_groups=groups, tiled=True)


def on_device(wave, projector, gvec, atom_of, dion, qaug):
    b, c = lax.axis_index("band"), lax.axis_index("coef")
    x, y, core, z_hi = b >> 3, (b >> 1) & 3, b & 1, c >> 3
    order = [y, (y + 3 + 2 * core) & 3, (y + 1 + 2 * core) & 3, (y + 2) & 3]
    place = jnp.stack(
        [core, z_hi] + [x * 4 + at for at in order] + [(1 - x) * 4 + at for at in order]).astype(jnp.int32)

    across = to_other_x(projector)
    before, after = ring(projector), against_ring(projector)
    far = ring(before)
    stat, wave_v = stats(wave, gvec)
    wave_other = swap(wave)
    across, after, far, stat, late_dion = lax.optimization_barrier((across, after, far, stat, dion))
    far_x = to_other_x(far)
    before_x, after_x = ring(across), against_ring(across)
    shards = [projector, before, after, far, across, before_x, after_x, far_x]
    weights = masked_weights(atom_of, late_dion, qaug)
    stat, weights = lax.optimization_barrier((stat, weights))
    message, whole = intersect(place, stat, wave_v, wave_other, shards)

    keep, message = near_sum(place, near_exchange(message))
    coupled = near_exchange(couple(place, keep, far_exchange(message), weights))
    return finish(place, coupled, wave_v, gvec, whole, swap(whole))


def solution(mesh):
    in_specs = (P("band", "coef"), P("band", "coef"), P(None, "coef"), P(), P(), P())
    out_specs = P("band", "coef")
    return jax.shard_map(
        on_device, mesh=mesh, in_specs=in_specs, out_specs=out_specs, check_vma=False
    )
```

```python
import functools
import jax
import jax.numpy as jnp
from jax import lax
from jax.experimental import pallas as pl
from jax.experimental.pallas import tpu as pltpu
from jax.sharding import PartitionSpec as P

kinetic_unit = 0.005
f32 = jnp.float32
bf16 = jnp.bfloat16

N_COEF = 32
N_BAND = 16
ROWS = 256
COLS = 4096
NPROJ = 512
SHARD = NPROJ // N_BAND
HALF_PROJ = NPROJ // 2
QUARTER_PROJ = NPROJ // 4
NEAR = 8
BANDS = ROWS // NEAR
STAT_ROWS = BANDS // 4
NEAR_ROWS = 2 * BANDS + STAT_ROWS
FAR_ROWS = BANDS + STAT_ROWS
N_Z_HI = N_COEF // NEAR
FAR = 2 * N_Z_HI

anywhere = pl.BlockSpec(memory_space=pl.ANY)
vmem = pl.BlockSpec(memory_space=pltpu.VMEM)
smem = pl.BlockSpec(memory_space=pltpu.SMEM)

CORE, Z_HI, ORDER = 0, 1, 2


def in_vmem(value):
    return pltpu.with_memory_space_constraint(value, pltpu.VMEM)


def in_hbm(value):
    return pltpu.with_memory_space_constraint(value, pltpu.HBM)


def params(mib):
    return pltpu.CompilerParams(vmem_limit_bytes=mib * 1024 * 1024)


def cost(flops, bytes_accessed):
    return pl.CostEstimate(flops=flops, bytes_accessed=bytes_accessed, transcendentals=0)


def pieces(value):
    hi = value.astype(bf16).astype(f32)
    rest = value - hi
    mid = rest.astype(bf16).astype(f32)
    lo = (rest - mid).astype(bf16).astype(f32)
    return hi, mid, lo


def stat_lanes():
    return lax.broadcasted_iota(jnp.int32, (STAT_ROWS, HALF_PROJ), 1)


def split_rows(value):
    lane = stat_lanes() & 63
    hi, mid, lo = [jnp.where((lane == 0) | (lane == 3), piece, 0.0) for piece in pieces(value)]
    return hi + pltpu.roll(mid, 1, 1) + pltpu.roll(lo, 2, 1)


def join_rows(packed):
    return packed + pltpu.roll(packed, HALF_PROJ - 1, 1) + pltpu.roll(packed, HALF_PROJ - 2, 1)


def to_rows(first, second):
    lane = stat_lanes()
    out = jnp.zeros((STAT_ROWS, HALF_PROJ), f32)
    for k in range(4):
        rows = slice(k * STAT_ROWS, (k + 1) * STAT_ROWS)
        out = jnp.where(lane == 64 * k, first[rows], jnp.where(lane == 64 * k + 3, second[rows], out))
    return split_rows(out)


def from_rows(packed):
    lane = stat_lanes()
    columns = []
    for begin in (0, 3):
        columns.append(jnp.concatenate([
            jnp.sum(jnp.where((lane >= 64 * k + begin) & (lane < 64 * k + begin + 3), packed, 0.0), axis=1, keepdims=True)
            for k in range(4)
        ], axis=0))
    return columns


def kinetic(gvec):
    comps = gvec.astype(f32)
    return kinetic_unit * (comps[0:1] * comps[0:1] + comps[1:2] * comps[1:2] + comps[2:3] * comps[2:3])


def stats_kernel(wave, gvec, stat, wave_v, sems):
    copies = [
        pltpu.make_async_copy(
            wave.at[pl.ds(n * BANDS, BANDS), :], wave_v.at[pl.ds(n * BANDS, BANDS), :], sems.at[n])
        for n in range(NEAR)
    ]
    for copy in copies:
        copy.start()
    kin = kinetic(gvec[...])
    for n, copy in enumerate(copies):
        copy.wait()
        value = wave_v[n * BANDS:(n + 1) * BANDS, :].astype(f32)
        square = value * value
        sq = jnp.sum(square, axis=1, keepdims=True)
        ksq = jnp.sum(square * kin, axis=1, keepdims=True)
        stat[n * STAT_ROWS:(n + 1) * STAT_ROWS, :] = to_rows(sq, ksq)


def stats(wave, gvec):
    return pl.pallas_call(
        stats_kernel,
        in_specs=[anywhere, vmem],
        out_specs=[vmem, vmem],
        out_shape=[
            jax.ShapeDtypeStruct((NEAR * STAT_ROWS, HALF_PROJ), f32),
            pltpu.VMEM((ROWS, COLS), bf16),
        ],
        scratch_shapes=[pltpu.SemaphoreType.DMA((NEAR,))],
        compiler_params=params(16),
        cost_estimate=cost(5 * ROWS * COLS, 2 * ROWS * COLS),
        name="stats",
    )(in_hbm(wave), gvec)


def weights_kernel(atom_of, dion, qaug, out):
    number = lax.broadcasted_iota(jnp.int32, (64, NPROJ), 0)
    member = jnp.where(atom_of[...] == number, 1.0, 0.0).astype(bf16)
    same = lax.dot_general(member, member, (((0,), (0,)), ((), ())), preferred_element_type=f32) > 0.5
    to = lax.broadcasted_iota(jnp.int32, (NPROJ, NPROJ), 0)
    source = ((to & 0xE0) << 1) | ((to >> 8) << 5) | (to & 31)
    order = jnp.where(source == lax.broadcasted_iota(jnp.int32, (NPROJ, NPROJ), 1), 1.0, 0.0).astype(bf16)
    for at, matrix in enumerate((dion, qaug)):
        value = jnp.where(same, matrix[...].astype(f32), 0.0).astype(bf16)
        rows = jnp.dot(order, value, preferred_element_type=f32).astype(bf16)
        out[:, at * NPROJ:(at + 1) * NPROJ] = lax.dot_general(
            rows, order, (((1,), (1,)), ((), ())), preferred_element_type=f32).astype(bf16)


def masked_weights(atom_of, dion, qaug):
    return pl.pallas_call(
        weights_kernel,
        in_specs=[vmem] * 3,
        out_specs=vmem,
        out_shape=jax.ShapeDtypeStruct((NPROJ, 2 * NPROJ), bf16),
        compiler_params=params(24),
        cost_estimate=cost(9 * NPROJ ** 3, 8 * NPROJ * NPROJ),
        name="masked_weights",
    )(atom_of.reshape(1, NPROJ), in_hbm(dion), in_hbm(qaug))


def against(left, right):
    return lax.dot_general(left, right, (((1,), (1,)), ((), ())), preferred_element_type=f32)


N_SHARDS = HALF_PROJ // SHARD


def intersect_kernel(place, stat, wave_own, wave_other, *refs):
    shards = refs[:N_SHARDS]
    message, whole, whole_v, message_v, out_sem = refs[N_SHARDS:]
    for i, shard in enumerate(shards):
        at = pl.multiple_of(place[ORDER + i] * SHARD, SHARD)
        whole_v[pl.ds(at, SHARD), :] = shard[...]
    back = pltpu.make_async_copy(whole_v, whole, out_sem)
    back.start()
    for core, wave in enumerate((wave_own, wave_other)):
        total = against(wave[...], whole_v[...])
        for n in range(NEAR):
            at = n * NEAR_ROWS + core * BANDS
            message_v[at:at + BANDS, :] = total[n * BANDS:(n + 1) * BANDS]
    for n in range(NEAR):
        at = n * NEAR_ROWS + 2 * BANDS
        message_v[at:at + STAT_ROWS, :] = stat[n * STAT_ROWS:(n + 1) * STAT_ROWS, :]
    message[...] = message_v[...].astype(bf16)
    back.wait()


def intersect(place, stat, wave_own, wave_other, shards):
    return pl.pallas_call(
        intersect_kernel,
        in_specs=[smem] + [vmem] * (3 + N_SHARDS),
        out_specs=[vmem, anywhere],
        out_shape=[
            jax.ShapeDtypeStruct((NEAR * NEAR_ROWS, HALF_PROJ), bf16),
            pltpu.HBM((HALF_PROJ, COLS), bf16),
        ],
        scratch_shapes=[
            pltpu.VMEM((HALF_PROJ, COLS), bf16),
            pltpu.VMEM((NEAR * NEAR_ROWS, HALF_PROJ), f32),
            pltpu.SemaphoreType.DMA,
        ],
        compiler_params=params(24),
        cost_estimate=cost(4 * ROWS * COLS * HALF_PROJ, 2 * (2 * ROWS + 2 * HALF_PROJ) * COLS),
        name="intersect",
    )(place, stat, in_vmem(wave_own), in_vmem(wave_other), *[in_vmem(shard) for shard in shards])


def near_sum_kernel(place, received, keep, message, message_v):
    total = jnp.sum(received[...].astype(f32).reshape(NEAR, NEAR_ROWS, HALF_PROJ), axis=0)
    keep[...] = total[:BANDS]
    rows = split_rows(join_rows(total[2 * BANDS:]))
    core = place[CORE]
    for zh in range(N_Z_HI):
        for c, value in ((core, total[:BANDS]), (1 - core, total[BANDS:2 * BANDS])):
            at = pl.multiple_of((zh * 2 + c) * FAR_ROWS, STAT_ROWS)
            message_v[pl.ds(at, BANDS), :] = value
            message_v[pl.ds(at + BANDS, STAT_ROWS), :] = rows
    message[...] = message_v[...].astype(bf16)


def near_sum(place, received):
    return pl.pallas_call(
        near_sum_kernel,
        in_specs=[smem, vmem],
        out_specs=[vmem, vmem],
        out_shape=[
            jax.ShapeDtypeStruct((BANDS, HALF_PROJ), f32),
            jax.ShapeDtypeStruct((FAR * FAR_ROWS, HALF_PROJ), bf16),
        ],
        scratch_shapes=[pltpu.VMEM((FAR * FAR_ROWS, HALF_PROJ), f32)],
        compiler_params=params(16),
        cost_estimate=cost(NEAR * NEAR_ROWS * HALF_PROJ, 3 * NEAR * NEAR_ROWS * HALF_PROJ),
        name="near_sum",
    )(place, received)


def couple_kernel(place, keep, received, weights, out):
    blocks = received[...].astype(f32).reshape(FAR, FAR_ROWS, HALF_PROJ)
    core = place[CORE]
    own_at = place[Z_HI] * 2 + core
    halves, packed = [], []
    for c in range(2):
        total = jnp.zeros((BANDS, HALF_PROJ), f32)
        rows = jnp.zeros((STAT_ROWS, HALF_PROJ), f32)
        for zh in range(N_Z_HI):
            block = blocks[zh * 2 + c]
            total += jnp.where(own_at == zh * 2 + c, keep[...], block[:BANDS])
            rows += block[BANDS:]
        halves.append(total)
        packed.append(rows)
    inter = jnp.concatenate(halves, axis=1)
    sq, ksq = from_rows(jnp.where(core == 0, packed[0], packed[1]))
    stacked = jnp.concatenate(pieces(inter), axis=0).astype(bf16)
    both = jnp.dot(stacked, weights[...], preferred_element_type=f32)
    both = both[:BANDS] + (both[BANDS:2 * BANDS] + both[2 * BANDS:])
    pd, pq = both[:, :NPROJ], both[:, NPROJ:]
    energy = (ksq + jnp.sum(inter * pd, axis=1, keepdims=True)) / (
        sq + jnp.sum(inter * pq, axis=1, keepdims=True))
    ekin = ksq / (sq + 1e-6)
    coupled = pd - energy * pq
    block = jnp.concatenate([coupled[:, :HALF_PROJ], coupled[:, HALF_PROJ:], to_rows(energy, ekin)], axis=0)
    out[...] = jnp.concatenate([block] * NEAR, axis=0).astype(bf16)


def couple(place, keep, received, weights):
    return pl.pallas_call(
        couple_kernel,
        in_specs=[smem] + [vmem] * 3,
        out_specs=vmem,
        out_shape=jax.ShapeDtypeStruct((NEAR * NEAR_ROWS, HALF_PROJ), bf16),
        compiler_params=params(16),
        cost_estimate=cost(12 * BANDS * NPROJ * NPROJ, 4 * NPROJ * NPROJ + 4 * ROWS * NPROJ),
        name="couple",
    )(place, keep, received, weights)


TILE = 512
PART = 256
N_TILES = COLS // TILE
CHUNK = 16


def finish_kernel(place, coupled, gvec, wave, whole_own, whole_other, out,
                  whole_v, out_v, halves_v, energy_v, scale_v, even_v, odd_v, sems, out_sems):
    def columns(tile):
        return pl.ds(pl.multiple_of(tile * TILE, TILE), TILE)

    def copies(tile):
        cols = columns(tile)
        return [
            pltpu.make_async_copy(
                source.at[:, cols], whole_v.at[pl.ds(i * HALF_PROJ, HALF_PROJ), cols], sems.at[tile, i])
            for i, source in enumerate((whole_own, whole_other))
        ]

    def out_copy(tile):
        cols = columns(tile)
        return pltpu.make_async_copy(out_v.at[:, cols], out.at[:, cols], out_sems.at[tile])

    def arrive(tile):
        for copy in copies(tile):
            copy.wait()

    def expand(tile, expanded_v):
        cols = columns(tile)
        expanded_v[...] = jnp.dot(halves_v[...], whole_v[:, cols], preferred_element_type=f32)

    def conclude(tile, expanded_v):
        for part in range(TILE // PART):
            cols = pl.ds(pl.multiple_of(tile * TILE + part * PART, PART), PART)
            kin = jnp.broadcast_to(kinetic(gvec[:, cols]), (CHUNK, PART))
            for i in range(ROWS // CHUNK):
                rows = slice(i * CHUNK, (i + 1) * CHUNK)
                energy = jnp.concatenate([energy_v[rows, :]] * (PART // 128), axis=1)
                scale = jnp.concatenate([scale_v[rows, :]] * (PART // 128), axis=1)
                expanded = expanded_v[rows, part * PART:(part + 1) * PART]
                resid = (kin - energy) * wave[rows, cols].astype(f32) + expanded
                t = kin * scale
                square = t * t
                num = (3.0 + t) * (9.0 + square)
                inverse = pl.reciprocal(num + square * square, approx=True)
                out_v[rows, cols] = ((num * inverse) * resid).astype(bf16)

    def depart(tiles):
        for tile in tiles:
            for copy in copies(tile):
                copy.start()

    depart(range(3))
    core = place[CORE]
    blocks = coupled[...].astype(f32).reshape(NEAR, NEAR_ROWS, HALF_PROJ)
    for n in range(NEAR):
        rows = slice(n * BANDS, (n + 1) * BANDS)
        first, second = blocks[n, :BANDS].astype(bf16), blocks[n, BANDS:2 * BANDS].astype(bf16)
        halves_v[rows, :HALF_PROJ] = jnp.where(core == 0, first, second)
        halves_v[rows, HALF_PROJ:] = jnp.where(core == 0, second, first)
        energy, ekin = from_rows(blocks[n, 2 * BANDS:])
        energy_v[rows, :] = jnp.broadcast_to(energy, (BANDS, 128))
        scale_v[rows, :] = jnp.broadcast_to(2.0 / ekin, (BANDS, 128))
    depart(range(3, N_TILES))
    arrive(0)
    expand(0, even_v)

    @pl.loop(0, N_TILES // 2)
    def _(i):
        arrive(2 * i + 1)

        @pl.when(i + 1 < N_TILES // 2)
        def _():
            arrive(2 * i + 2)

        expand(2 * i + 1, odd_v)
        conclude(2 * i, even_v)
        out_copy(2 * i).start()
        expand(jnp.minimum(2 * i + 2, N_TILES - 1), even_v)
        conclude(2 * i + 1, odd_v)
        out_copy(2 * i + 1).start()

    for tile in range(N_TILES):
        out_copy(tile).wait()


def finish(place, coupled, wave, gvec, whole_own, whole_other):
    return pl.pallas_call(
        finish_kernel,
        in_specs=[smem] + [vmem] * 3 + [anywhere] * 2,
        out_specs=anywhere,
        out_shape=jax.ShapeDtypeStruct((ROWS, COLS), bf16),
        scratch_shapes=[pltpu.VMEM((NPROJ, COLS), bf16), pltpu.VMEM((ROWS, COLS), bf16), pltpu.VMEM((ROWS, NPROJ), bf16)]
        + [pltpu.VMEM((ROWS, 128), f32)] * 2 + [pltpu.VMEM((ROWS, TILE), f32)] * 2
        + [pltpu.SemaphoreType.DMA((N_TILES, 2)), pltpu.SemaphoreType.DMA((N_TILES,))],
        compiler_params=params(24),
        cost_estimate=cost(2 * ROWS * COLS * NPROJ, 2 * (2 * ROWS + NPROJ) * COLS),
        name="finish",
    )(place, coupled, gvec, in_vmem(wave), in_hbm(whole_own), whole_other)


def band_perm(move):
    pairs = []
    for b in range(N_BAND):
        x, y, c = move(b // 8, (b // 2) % 4, b % 2)
        pairs.append((b, (x % 2) * 8 + (y % 4) * 2 + c))
    return pairs


def along_band(value, move):
    return lax.ppermute(value, "band", band_perm(move))


def swap(value):
    return along_band(value, lambda x, y, c: (x, y, 1 - c))


def ring(value):
    return along_band(value, lambda x, y, c: (x, y + 1 - 2 * c, c))


def against_ring(value):
    return along_band(value, lambda x, y, c: (x, y - 1 + 2 * c, c))


def to_other_x(value):
    return along_band(value, lambda x, y, c: (x + 1, y, c))


def near_exchange(value):
    groups = [[zh * NEAR + n for n in range(NEAR)] for zh in range(N_Z_HI)]
    return lax.all_to_all(value, "coef", 0, 0, axis_index_groups=groups, tiled=True)


def far_exchange(value):
    groups = [
        [(zh * NEAR + n) * N_BAND + chip * 2 + core for zh in range(N_Z_HI) for core in range(2)]
        for n in range(NEAR) for chip in range(N_BAND // 2)
    ]
    return lax.all_to_all(value, ("coef", "band"), 0, 0, axis_index_groups=groups, tiled=True)


def on_device(wave, projector, gvec, atom_of, dion, qaug):
    b, c = lax.axis_index("band"), lax.axis_index("coef")
    x, y, core, z_hi = b >> 3, (b >> 1) & 3, b & 1, c >> 3
    order = [y, (y + 3 + 2 * core) & 3, (y + 1 + 2 * core) & 3, (y + 2) & 3]
    place = jnp.stack(
        [core, z_hi] + [x * 4 + at for at in order] + [(1 - x) * 4 + at for at in order]).astype(jnp.int32)

    across = to_other_x(projector)
    before, after = ring(projector), against_ring(projector)
    far = ring(before)
    stat, wave_v = stats(wave, gvec)
    across, after, far, own_wave, stat, late_dion = lax.optimization_barrier((across, after, far, wave, stat, dion))
    far_x = to_other_x(far)
    before_x, after_x = ring(across), against_ring(across)
    wave_other = swap(own_wave)
    shards = [projector, before, after, far, across, before_x, after_x, far_x]
    weights = masked_weights(atom_of, late_dion, qaug)
    stat, weights = lax.optimization_barrier((stat, weights))
    message, whole = intersect(place, stat, wave_v, wave_other, shards)

    keep, message = near_sum(place, near_exchange(message))
    coupled = near_exchange(couple(place, keep, far_exchange(message), weights))
    return finish(place, coupled, wave_v, gvec, whole, swap(whole))


def solution(mesh):
    in_specs = (P("band", "coef"), P("band", "coef"), P(None, "coef"), P(), P(), P())
    out_specs = P("band", "coef")
    return jax.shard_map(
        on_device, mesh=mesh, in_specs=in_specs, out_specs=out_specs, check_vma=False
    )
```
